256 devices in a mesh: space: 16 (over y_lo, z), vel: 16 (over y_hi, x, core).
Axes of the slice: x: 4, y: 4 (y_hi: 2, y_lo: 2; y = y_hi * 2 + y_lo), z: 8, core: 2. Of those that a mesh axis runs over, the one named last changes fastest.
Arguments:
- dist: float32 [192, 4, 4, 32768], P('space', None, None, 'vel'), may hold values from 0.2 to 5
- cell_kind: int32 [192, 4, 4], P('space'), may hold values from 0 to 2
- inflow: float32 [32768], P('vel'), may hold values from 0.2 to 5
- wall_shape: float32 [32768], P('vel'), may hold values from 0.2 to 5
- gain_tables: float32 [1, 32768], replicated, may hold values from -6 to 6
- second_tables: float32 [1, 32768], replicated, may hold values from -6 to 6
Outputs:
- advanced: float32 [192, 4, 4, 32768], P('space', None, None, 'vel')
The draws below stay inside these ranges and needn't reach their ends.
Inputs may be any that keep to these rules, and one draw needn't show every extreme that they name: `cell_kind`: 0 marks a gas cell, 1 a wall cell, 2 an inflow cell.
All inputs are finite; a program needn't handle non-finite values.
Results may differ from the reference program's by a relative error of at most 0.0003.
Values sent between devices are 32-bit elements; how exact they have to be, the bound alone decides.
A program may use at most 192 MiB of HBM per device.

```python
import math
import jax
import jax.numpy as jnp
from jax import lax

VR = 32
NV = 32768
TERMS = 1
NY = 4
NZ = 4
NX = 192


def touch_ends(entries, key, smallest, high):
    extent = entries.shape
    index_at = [jax.random.randint(jax.random.fold_in(key, axis), (), 0, extent[axis]) for axis in range(len(extent))]
    entries = entries.at[tuple(index_at)].set(smallest)
    longest = extent.index(max(extent))
    index_at[longest] = (index_at[longest] + 1) % extent[longest]
    return entries.at[tuple(index_at)].set(high)


def block_scale(own_key, extent, pieces, smallest, largest):
    gain = 1.0
    for position, shards_of in pieces:
        steps = jax.random.uniform(jax.random.fold_in(jax.random.fold_in(own_key, 6), position), (shards_of,), jnp.float32, smallest / len(pieces), largest / len(pieces))
        gain = gain * jnp.repeat(jnp.exp(steps), extent[position] // shards_of).reshape((-1,) + (1,) * (len(extent) - 1 - position))
    return gain


def normal_values(stream_key, shape, width, most, kind=jnp.bfloat16):
    values = width * jax.random.normal(stream_key, shape, jnp.float32)
    return jnp.clip(values, min=-most, max=most).astype(kind)


def setup_inputs(seed: int = 0) -> dict:
    splits = jax.random.split(jax.random.key(seed), 7)
    dist = jnp.clip(jnp.exp(math.log(5.0) - 3.218876 * jax.random.uniform(splits[0], (NX, NY, NZ, NV), jnp.float32) ** block_scale(splits[0], (NX, NY, NZ, NV), ((0, 16), (3, 16)), -0.2, 0.2)), 0.2, 5.0)
    cell_kind = touch_ends(jax.random.randint(splits[1], (NX, NY, NZ), 0, 3), jax.random.fold_in(splits[1], 1), 0, 2).astype(jnp.int32)
    inflow = jnp.clip(jnp.exp(math.log(5.0) - 3.218876 * jax.random.uniform(splits[2], (NV,), jnp.float32) ** block_scale(splits[2], (NV,), ((0, 16),), -0.2, 0.2)), 0.2, 5.0)
    wall_shape = jnp.clip(jnp.exp(math.log(5.0) - 3.218876 * jax.random.uniform(splits[3], (NV,), jnp.float32) ** block_scale(splits[3], (NV,), ((0, 16),), -0.2, 0.2)), 0.2, 5.0)
    gain_tables = normal_values(splits[4], (TERMS, NV), 1.0, 6.0, jnp.float32)
    second_tables = normal_values(splits[5], (TERMS, NV), 1.0, 6.0, jnp.float32)
    return dict(dist=dist, cell_kind=cell_kind, inflow=inflow, wall_shape=wall_shape, gain_tables=gain_tables, second_tables=second_tables)


CFL = 0.3
COLLISION_AXIS = 0.25


def courant(index):
    first = index // (VR * VR)
    second = (index // VR) % VR
    third = index % VR
    return tuple(CFL * (2 * part - (VR - 1)).astype(jnp.float32) / (VR - 1) for part in (first, second, third))


def minmod(left, right):
    return 0.5 * (jnp.sign(left) + jnp.sign(right)) * jnp.minimum(jnp.abs(left), jnp.abs(right))


def cropped_field(array, lower, upper, axis):
    return lax.slice_in_dim(array, lower, array.shape[axis] - upper, axis=axis)


def face_terms(ext, speed, axis):
    left = cropped_field(ext, 0, 2, axis)
    middle = cropped_field(ext, 1, 1, axis)
    right = cropped_field(ext, 2, 0, axis)
    slope = minmod(middle - left, right - middle)
    upper = jnp.maximum(speed, 0.0)
    lower = jnp.minimum(speed, 0.0)
    flux = upper * (cropped_field(middle, 0, 1, axis) + 0.5 * (1.0 - upper) * cropped_field(slope, 0, 1, axis))
    flux = flux + lower * (cropped_field(middle, 1, 0, axis) - 0.5 * (1.0 + lower) * cropped_field(slope, 1, 0, axis))
    return cropped_field(flux, 1, 0, axis) - cropped_field(flux, 0, 1, axis)


def advect_cells(ext, speeds):
    core = ext[2:-2]
    change = face_terms(ext, speeds[0], 0)
    ext_y = jnp.concatenate([core[:, -2:], core, core[:, :2]], 1)
    change = change + face_terms(ext_y, speeds[1], 1)
    ext_z = jnp.concatenate([core[:, :, -2:], core, core[:, :, :2]], 2)
    change = change + face_terms(ext_z, speeds[2], 2)
    return core - change


def boundary(dist, cell_kind, inflow, wall_shape, scale):
    kind = cell_kind[..., None]
    walls = scale[..., None] * wall_shape
    return jnp.where(kind == 2, inflow, jnp.where(kind == 1, walls, dist))


def collide(cell_grid, gain_tables, second_tables):
    cell_count = cell_grid.shape[0]
    field = cell_grid.reshape(cell_count, VR, VR, VR)
    spectrum = jnp.fft.fftn(field, axes=(1, 2, 3))
    total_mass = jnp.zeros_like(field)
    for term in range(gain_tables.shape[0]):
        first = jnp.fft.ifftn(gain_tables[term].reshape(VR, VR, VR) * spectrum, axes=(1, 2, 3))
        second = jnp.fft.ifftn(second_tables[term].reshape(VR, VR, VR) * spectrum, axes=(1, 2, 3))
        total_mass = total_mass + (jnp.real(first) * jnp.real(second) - jnp.imag(first) * jnp.imag(second))
    return cell_grid + COLLISION_AXIS * total_mass.reshape(cell_count, -1)


def reference(dist, cell_kind, inflow, wall_shape, gain_tables, second_tables):
    total_v = dist.shape[3]
    rho = jnp.sum(dist, axis=3) / total_v
    wall_mean = jnp.sum(wall_shape) / total_v
    start = boundary(dist, cell_kind, inflow, wall_shape, rho / wall_mean)
    ext = jnp.pad(start, ((2, 2), (0, 0), (0, 0), (0, 0)))
    speeds = courant(jnp.arange(total_v, dtype=jnp.int32))
    read = advect_cells(ext, speeds)
    cell_grid = read.reshape(-1, total_v)
    number = cell_grid.shape[0]
    block = math.gcd(number, 32)
    result = lax.map(lambda piece: collide(piece, gain_tables, second_tables), cell_grid.reshape(number // block, block, total_v))
    return result.reshape(dist.shape)
```

```python
import functools
import math

import jax
import jax.numpy as jnp
import numpy as np
from jax import lax
from jax.experimental import pallas as pl
from jax.experimental.pallas import tpu as pltpu
from jax.sharding import PartitionSpec as P

VR = 32
NV = VR * VR * VR
CFL = 0.3
COLLISION_AXIS = 0.25
HIGH = lax.Precision.HIGHEST
MESH = pl.DeviceIdType.MESH
F32 = jnp.float32
BF16 = jnp.bfloat16

FULL = 136
HALF = 128
PAIR = 2

ORDER = (
    (1, 0, 0), (0, 1, 0), (0, 3, 1), (1, 2, 0), (1, 1, 0), (1, 3, 1), (0, 2, 0), (1, 0, 1),
    (0, 1, 1), (0, 3, 0), (1, 2, 1), (1, 1, 1), (1, 3, 0), (0, 2, 1), (0, 0, 1),
)


def halves(table):
    high = jnp.asarray(table, F32).astype(BF16)
    low = (jnp.asarray(table, F32) - high.astype(F32)).astype(BF16)
    return high, low


def np_halves(table):
    table = np.asarray(table, np.float32)
    high = table.astype(BF16)
    low = (table - high.astype(np.float32)).astype(BF16)
    return high, low


def tables():
    two_pi = 2.0 * math.pi
    row = np.arange(256)
    a, b_hi = row // 8, row % 8
    spec = np.arange(FULL)
    ka = np.where(spec < HALF, spec % 16, 16)
    r = np.where(spec < HALF, spec // 16, spec - HALF)
    theta = two_pi / 32 * ((ka[:, None] * a[None] + 4 * r[:, None] * b_hi[None]) % 32)
    left = np.concatenate([np.cos(theta), -np.sin(theta)], 0)
    lane = np.arange(128)
    b_lo, c = lane // 32, lane % 32
    angle = two_pi / 32 * ((8 * b_lo[:, None] * b_lo[None] + c[:, None] * c[None]) % 32)
    cos, sin = np.cos(angle), np.sin(angle)
    right = np.block([[cos, -sin], [sin, cos]])
    back = np.block([[cos, sin], [-sin, cos]])
    turn = two_pi / 32 * (r[:, None] * b_lo[None])
    twiddle = np.stack([np.cos(turn), np.sin(turn)])
    th = theta[:HALF].T
    phi = two_pi / 8 * ((r[None, :HALF] * b_hi[:, None]) % 8)
    sign = np.where(a % 2 == 0, 1.0, -1.0)[:, None]
    first = (ka[:HALF] == 0)[None]
    real = np.where(first, np.cos(phi) + sign * np.sin(phi), 2 * np.cos(th))
    imag = np.where(first, -np.sin(phi) + sign * np.cos(phi), -2 * np.sin(th))
    out = np.concatenate([real, imag], 1)
    source = ((-a) % 32) * 8
    flip0 = np.zeros((256, 256), np.float32)
    flip0[row, source + (-b_hi) % 8] = 1
    flip1 = np.zeros((256, 256), np.float32)
    flip1[row, source + (-b_hi - 1) % 8] = 1
    flip_lane = np.zeros((128, 128), np.float32)
    flip_lane[((-b_lo) % 4) * 32 + (-c) % 32, lane] = 1
    flips = np.concatenate([flip0, flip1], 0)
    mats = []
    for table in (left, right, back, out):
        mats += list(np_halves(table))
    return mats, twiddle.astype(np.float32), flips, flip_lane


def split(value):
    high = value.astype(BF16)
    return high, (value - high.astype(F32)).astype(BF16)


def mul3(left, right):
    dot = functools.partial(jnp.dot, preferred_element_type=F32)
    return dot(left[0], right[0]) + (dot(left[1], right[0]) + dot(left[0], right[1]))


def minmod(p, q):
    return jnp.maximum(jnp.minimum(p, q), jnp.minimum(jnp.maximum(p, q), 0.0))


def coords(vel):
    return vel // 8, (vel // 2) % 4, vel % 2


def partner(vel, off):
    y, x, core = coords(vel)
    return ((y + off[0]) % 2) * 8 + ((x + off[1]) % 4) * 2 + (core + off[2]) % 2


def step_kernel(
    spaces, layers,
    dist, kind, inflow, wall, gain, second, lh, ll, rh, rl, bh, bl, oh, ol, twiddle, flips, flip_lane,
    result,
    ext, lane_sums, mass_row, mass_all, scales, read, cells, done, nat, weights, weights16, yh, yl, vh, vl,
    in_sem, mass_send, mass_recv, halo_send, halo_recv, go_send, go_recv, back_send, back_recv, own_sem,
):
    sp = lax.axis_index("space")
    me = lax.axis_index("vel")
    my_y, my_z = me // 4, me % 4
    chunks = layers // PAIR
    count = layers * 16

    loads = []
    for l in range(16):
        loads.append(pltpu.make_async_copy(
            dist.at[:, :, :, pl.ds(128 * l, 128)],
            ext.at[pl.ds(2, layers), :, :, l, :],
            in_sem.at[l],
        ))
        loads[-1].start()

    barrier = pltpu.get_barrier_semaphore()
    for off in ORDER:
        pl.semaphore_signal(barrier, inc=1, device_id=(sp, partner(me, off)), device_id_type=MESH)
    for near in (1, spaces - 1):
        pl.semaphore_signal(barrier, inc=1, device_id=(lax.rem(sp + near, spaces), me), device_id_type=MESH)

    lane_sums[...] = jnp.zeros_like(lane_sums)
    lane_sums[count:count + 8, :] = jnp.concatenate(
        [jnp.sum(wall[...], axis=0, keepdims=True), jnp.zeros((7, 128), F32)], 0)
    for load in loads:
        load.wait()

    def sum_layer(x, _):
        block = ext[2 + x].reshape(16, 2, 8, 128)
        block = jnp.sum(block[:, 0] + block[:, 1], axis=1)
        lane_sums[pl.ds(pl.multiple_of(x * 16, 16), 16), :] = block
        return 0

    lax.fori_loop(0, layers, sum_layer, 0)
    mass_row[...] = jnp.sum(lane_sums[...].T, axis=0, keepdims=True)
    mass_all[me] = mass_row[...]

    pl.semaphore_wait(barrier, len(ORDER) + 2)

    sends = []
    for i, off in enumerate(ORDER):
        sends.append(pltpu.make_async_remote_copy(
            src_ref=mass_row, dst_ref=mass_all.at[me], send_sem=mass_send.at[i], recv_sem=mass_recv.at[i],
            device_id=(sp, partner(me, off)), device_id_type=MESH,
        ))
        sends[-1].start()

    lane = lax.broadcasted_iota(jnp.int32, (16, 128), 1) // 32
    sub = lax.broadcasted_iota(jnp.int32, (8, 128), 0)
    lane8 = lax.broadcasted_iota(jnp.int32, (8, 128), 1) // 32
    for t, (table, scale) in enumerate(((gain, 1.0 / NV), (second, COLLISION_AXIS / NV))):
        g = table[...]
        rev = jnp.dot(g, flip_lane[...], precision=HIGH, preferred_element_type=F32)
        mask = lax.broadcasted_iota(jnp.int32, (256, 128), 1) < 32
        rev0 = jnp.dot(flips[0:256, :], rev, precision=HIGH, preferred_element_type=F32)
        rev1 = jnp.dot(flips[256:512, :], rev, precision=HIGH, preferred_element_type=F32)
        rev = jnp.where(mask, rev0, rev1)
        nat[2 * t] = (0.5 * scale) * (g + rev)
        nat[2 * t + 1] = (0.5 * scale) * (g - rev)

    def order_weights(t, _):
        for r in range(8):
            high, low = r // 4, r % 4
            value = jnp.zeros((16, 128), F32)
            value16 = jnp.zeros((8, 128), F32)
            for q in range(4):
                rows = nat[t, pl.ds(2 * q + high, 16, stride=8), :]
                row16 = jnp.broadcast_to(nat[t, pl.ds(128 + 2 * q + high, 1), :], (8, 128))
                shift = (32 * (q - low)) % 128
                if shift:
                    rows = pltpu.roll(rows, shift, 1)
                    row16 = pltpu.roll(row16, shift, 1)
                value = jnp.where(lane == q, rows, value)
                value16 = jnp.where(lane8 == q, row16, value16)
            weights[t, 16 * r:16 * r + 16, :] = value
            weights16[t, 8 * r:8 * r + 8, :] = jnp.where(sub == 0, value16, 0.0)
        return 0

    lax.fori_loop(0, 4, order_weights, 0)

    for copy in sends:
        copy.wait()
    total = jnp.sum(mass_all[...], axis=0)
    totals = jnp.broadcast_to(total, (128, 256)).T
    scales[...] = totals[:count] / totals[count:count + 1]

    def boundary_layer(x, _):
        for y in range(4):
            for z in range(4):
                what = jnp.full((8, 128), kind[x, y, z], jnp.int32)
                scale = jnp.broadcast_to(scales[pl.ds(x * 16 + 4 * y + z, 1), :], (8, 128))
                for e in range(2):
                    rows = slice(8 * e, 8 * e + 8)
                    value = jnp.where(what == 1, scale * wall[rows, :], ext[2 + x, y, z, rows, :])
                    ext[2 + x, y, z, rows, :] = jnp.where(what == 2, inflow[rows, :], value)
        return 0

    lax.fori_loop(0, 2, boundary_layer, 0)
    lax.fori_loop(layers - 2, layers, boundary_layer, 0)
    to_left = pltpu.make_async_remote_copy(
        src_ref=ext.at[pl.ds(2, 2)], dst_ref=ext.at[pl.ds(layers + 2, 2)],
        send_sem=halo_send.at[0], recv_sem=halo_recv.at[0],
        device_id=(lax.rem(sp + spaces - 1, spaces), me), device_id_type=MESH)
    to_right = pltpu.make_async_remote_copy(
        src_ref=ext.at[pl.ds(layers, 2)], dst_ref=ext.at[pl.ds(0, 2)],
        send_sem=halo_send.at[1], recv_sem=halo_recv.at[1],
        device_id=(lax.rem(sp + 1, spaces), me), device_id_type=MESH)

    @pl.when(sp > 0)
    def _():
        to_left.start()

    @pl.when(sp < spaces - 1)
    def _():
        to_right.start()

    @pl.when(sp == 0)
    def _():
        ext[0:2] = jnp.zeros((2, 4, 4, 16, 128), F32)

    @pl.when(sp == spaces - 1)
    def _():
        ext[layers + 2:layers + 4] = jnp.zeros((2, 4, 4, 16, 128), F32)

    lax.fori_loop(2, layers - 2, boundary_layer, 0)

    b_index = 4 * lax.broadcasted_iota(jnp.int32, (8, 128), 0) + lane8
    c_index = lax.broadcasted_iota(jnp.int32, (8, 128), 1) % 32

    def speed(index):
        return CFL * (2 * index - (VR - 1)).astype(F32) / (VR - 1)

    nu_y, nu_z = speed(b_index), speed(c_index)
    up_y, up_z = nu_y > 0, nu_z > 0
    size_y, size_z = jnp.abs(nu_y), jnp.abs(nu_z)
    coef_y = jnp.where(up_y, 0.5, -0.5) * (1.0 - size_y)
    coef_z = jnp.where(up_z, 0.5, -0.5) * (1.0 - size_z)

    def ring(s, coef, up, size):
        diff = [s[(i + 1) % 4] - s[i] for i in range(4)]
        face = [s[i] + coef * minmod(diff[i - 1], diff[i]) for i in range(4)]
        step = [face[(i + 1) % 4] - face[i] for i in range(4)]
        return [size * jnp.where(up, step[i - 1], -step[i]) for i in range(4)]

    def transport(x0):
        for e in range(2):
            rows = slice(8 * e, 8 * e + 8)
            nu_x = speed(jnp.full((8, 128), 2 * me + e, jnp.int32))
            up_x = nu_x > 0
            size_x = jnp.abs(nu_x)
            coef_x = jnp.where(up_x, 0.5, -0.5) * (1.0 - size_x)
            for y in range(4):
                for z in range(4):
                    s = [ext[x0 + i, y, z, rows, :] for i in range(6)]
                    diff = [s[i + 1] - s[i] for i in range(5)]
                    face = [s[i + 1] + coef_x * minmod(diff[i], diff[i + 1]) for i in range(4)]
                    step = [face[i + 1] - face[i] for i in range(3)]
                    for i in range(PAIR):
                        read[x0 + i, 4 * y + z, rows, :] = s[i + 2] - size_x * jnp.where(up_x, step[i], -step[i + 1])
            for i in range(PAIR):
                s = [[ext[x0 + 2 + i, y, z, rows, :] for z in range(4)] for y in range(4)]
                along_z = [ring(s[y], coef_z, up_z, size_z) for y in range(4)]
                along_y = [ring([s[y][z] for y in range(4)], coef_y, up_y, size_y) for z in range(4)]
                for y in range(4):
                    for z in range(4):
                        read[x0 + i, 4 * y + z, rows, :] -= along_z[y][z] + along_y[z][y]

    own = pl.ds(pl.multiple_of(16 * me, 16), 16)

    def send_chunk(k, x0):
        transport(x0)
        for i in range(PAIR):
            cells[x0 + i, own, :] = read[x0 + i, me]
        for off in ORDER:
            to = partner(me, off)
            pltpu.make_async_remote_copy(
                src_ref=read.at[pl.ds(x0, PAIR), to], dst_ref=cells.at[pl.ds(x0, PAIR), own, :],
                send_sem=go_send.at[k], recv_sem=go_recv.at[k],
                device_id=(sp, to), device_id_type=MESH,
            ).start()

    def first_of(k):
        return lax.rem(PAIR * k + 2, layers)

    def inner(k, _):
        send_chunk(k, first_of(k))
        return 0

    lax.fori_loop(0, chunks - 2, inner, 0)

    @pl.when(sp > 0)
    def _():
        to_right.wait_recv()

    @pl.when(sp < spaces - 1)
    def _():
        to_left.wait_recv()

    lax.fori_loop(chunks - 2, chunks, inner, 0)

    def collide(k, _):
        x0 = first_of(k)
        arrived = cells.at[pl.ds(x0, PAIR), pl.ds(0, 240), :]
        pltpu.make_async_copy(arrived, arrived, go_recv.at[k]).wait()
        field = jnp.concatenate([cells[x0], cells[x0 + 1]], 1)
        spec = mul3((lh[...], ll[...]), split(field))
        tc, ts = twiddle[0], twiddle[1]
        parts = []
        for i in range(PAIR):
            re = spec[:FULL, 128 * i:128 * i + 128]
            im = spec[FULL:, 128 * i:128 * i + 128]
            parts.append(jnp.concatenate([re * tc + im * ts, im * tc - re * ts], 1))
        spec = mul3(split(jnp.concatenate(parts, 0)), (rh[...], rl[...]))
        tc, ts = twiddle[0, :HALF, :], twiddle[1, :HALF, :]
        for i in range(PAIR):
            re = spec[FULL * i:FULL * i + HALF, :128].reshape(8, 16, 128)
            im = spec[FULL * i:FULL * i + HALF, 128:].reshape(8, 16, 128)
            re16 = spec[FULL * i + HALF:FULL * (i + 1), :128]
            im16 = spec[FULL * i + HALF:FULL * (i + 1), 128:]
            for t in range(4):
                w = weights[t].reshape(8, 16, 128)
                for r in range(8):
                    w16 = weights16[t, 8 * r:8 * r + 8, :]
                    zr, zi = w[r] * re[r], w[r] * im[r]
                    zr = jnp.concatenate([zr[:8] - w16 * im16[r:r + 1, :], zr[8:]], 0)
                    zi = jnp.concatenate([zi[:8] + w16 * re16[r:r + 1, :], zi[8:]], 0)
                    if t % 2:
                        zr, zi = zi, -zr
                    rows = slice(HALF * (PAIR * t + i) + 16 * r, HALF * (PAIR * t + i) + 16 * r + 16)
                    high, low = split(jnp.concatenate([zr, zi], 1))
                    yh[rows, :] = high
                    yl[rows, :] = low
        fields = []
        for t in range(4):
            rows = slice(PAIR * HALF * t, PAIR * HALF * (t + 1))
            value = mul3((yh[rows, :], yl[rows, :]), (bh[...], bl[...]))
            reals, imags = [], []
            for i in range(PAIR):
                re = value[HALF * i:HALF * (i + 1), :128]
                im = value[HALF * i:HALF * (i + 1), 128:]
                reals.append(re * tc - im * ts)
                imags.append(re * ts + im * tc)
            value = jnp.concatenate([jnp.concatenate(reals, 1), jnp.concatenate(imags, 1)], 0)
            fields.append(mul3((oh[...], ol[...]), split(value)))
        value = fields[0] * fields[2] - fields[1] * fields[3]
        for i in range(PAIR):
            done[x0 + i] = cells[x0 + i] + value[:, 128 * i:128 * i + 128]
        for off in ORDER:
            to = partner(me, off)
            pltpu.make_async_remote_copy(
                src_ref=done.at[pl.ds(x0, PAIR), pl.ds(pl.multiple_of(16 * to, 16), 16), :],
                dst_ref=result.at[pl.ds(x0, PAIR), my_y, my_z],
                send_sem=back_send.at[k], recv_sem=back_recv.at[k],
                device_id=(sp, to), device_id_type=MESH,
            ).start()
        return 0

    lax.fori_loop(0, chunks, collide, 0)

    mine = pltpu.make_async_copy(
        done.at[:, own, :], result.at[:, my_y, my_z], own_sem)
    mine.start()

    def finish(k, _):
        x0 = first_of(k)
        block = cells.at[pl.ds(x0, PAIR), pl.ds(0, 240), :]
        pltpu.make_async_copy(block, block, go_send.at[k]).wait()
        pltpu.make_async_copy(block, block, back_send.at[k]).wait()
        pltpu.make_async_copy(block, block, back_recv.at[k]).wait()
        return 0

    lax.fori_loop(0, chunks, finish, 0)
    mine.wait()

    @pl.when(sp > 0)
    def _():
        to_left.wait_send()

    @pl.when(sp < spaces - 1)
    def _():
        to_right.wait_send()


def place_kernel(source, target, sem):
    copies = []
    for l in range(16):
        copies.append(pltpu.make_async_copy(
            source.at[:, :, :, l, :], target.at[:, :, :, pl.ds(128 * l, 128)], sem.at[l]))
        copies[-1].start()
    for copy in copies:
        copy.wait()


def shards(spaces, dist, cell_kind, inflow, wall_shape, gain_tables, second_tables):
    layers = dist.shape[0]
    mats, twiddle, flips, flip_lane = tables()
    vmem = pl.BlockSpec(memory_space=pltpu.VMEM)
    anywhere = pl.BlockSpec(memory_space=pl.ANY)
    chunks = layers // PAIR
    dma = pltpu.SemaphoreType.DMA
    result = pl.pallas_call(
        functools.partial(step_kernel, spaces, layers),
        out_shape=jax.ShapeDtypeStruct((layers, 4, 4, 16, 128), F32),
        in_specs=[anywhere, pl.BlockSpec(memory_space=pltpu.SMEM)] + [vmem] * 15,
        out_specs=anywhere,
        scratch_shapes=[
            pltpu.VMEM((layers + 4, 4, 4, 16, 128), F32),
            pltpu.VMEM((256, 128), F32),
            pltpu.VMEM((1, 256), F32),
            pltpu.VMEM((16, 1, 256), F32),
            pltpu.VMEM((layers * 16, 128), F32),
            pltpu.VMEM((layers, 16, 16, 128), F32),
            pltpu.VMEM((layers, 256, 128), F32),
            pltpu.VMEM((layers, 256, 128), F32),
            pltpu.VMEM((4, 256, 128), F32),
            pltpu.VMEM((4, HALF, 128), F32),
            pltpu.VMEM((4, 64, 128), F32),
            pltpu.VMEM((4 * PAIR * HALF, 256), BF16),
            pltpu.VMEM((4 * PAIR * HALF, 256), BF16),
            pltpu.VMEM((16, 128), BF16),
            pltpu.VMEM((16, 128), BF16),
            dma((16,)),
            dma((15,)), dma((15,)),
            dma((2,)), dma((2,)),
            dma((chunks,)), dma((chunks,)),
            dma((chunks,)), dma((chunks,)),
            dma,
        ],
        compiler_params=pltpu.CompilerParams(
            collective_id=0, has_side_effects=True, vmem_limit_bytes=32 * 2**20),
    )(
        dist, cell_kind, inflow.reshape(16, 128), wall_shape.reshape(16, 128),
        gain_tables.reshape(256, 128), second_tables.reshape(256, 128),
        *[jnp.asarray(m) for m in mats], jnp.asarray(twiddle), jnp.asarray(flips), jnp.asarray(flip_lane),
    )
    return pl.pallas_call(
        place_kernel,
        out_shape=jax.ShapeDtypeStruct(dist.shape, F32),
        in_specs=[anywhere],
        out_specs=anywhere,
        scratch_shapes=[dma((16,))],
    )(result)


def solution(mesh):
    placed = (P("space", None, None, "vel"), P("space", None, None), P("vel"), P("vel"), P(), P())
    return jax.shard_map(
        functools.partial(shards, mesh.shape["space"]),
        mesh=mesh, in_specs=placed, out_specs=P("space", None, None, "vel"), check_vma=False,
    )
```

```python
import functools
import math

import jax
import jax.numpy as jnp
import numpy as np
from jax import lax
from jax.experimental import pallas as pl
from jax.experimental.pallas import tpu as pltpu
from jax.sharding import PartitionSpec as P

VR = 32
NV = VR * VR * VR
CFL = 0.3
COLLISION_AXIS = 0.25
HIGH = lax.Precision.HIGHEST
MESH = pl.DeviceIdType.MESH
F32 = jnp.float32
BF16 = jnp.bfloat16

FULL = 136
HALF = 128
PAIR = 2

ORDER = (
    (1, 0, 0), (0, 1, 0), (0, 3, 1), (1, 2, 0), (1, 1, 0), (1, 3, 1), (0, 2, 0), (1, 0, 1),
    (0, 1, 1), (0, 3, 0), (1, 2, 1), (1, 1, 1), (1, 3, 0), (0, 2, 1), (0, 0, 1),
)


def tables():
    two_pi = 2.0 * math.pi
    row = np.arange(256)
    a, b_hi = row // 8, row % 8
    spec = np.arange(FULL)
    ka = np.where(spec < HALF, spec % 16, 16)
    r = np.where(spec < HALF, spec // 16, spec - HALF)
    theta = two_pi / 32 * ((ka[:, None] * a[None] + 4 * r[:, None] * b_hi[None]) % 32)
    left = np.concatenate([np.cos(theta), -np.sin(theta)], 0)
    lane = np.arange(128)
    b_lo, c = lane // 32, lane % 32
    angle = two_pi / 32 * ((8 * b_lo[:, None] * b_lo[None] + c[:, None] * c[None]) % 32)
    cos, sin = np.cos(angle), np.sin(angle)
    right = np.block([[cos, -sin], [sin, cos]])
    back = np.block([[cos, sin], [-sin, cos]])
    turn = two_pi / 32 * (r[:, None] * b_lo[None])
    twiddle = np.stack([np.cos(turn), np.sin(turn)])
    th = theta[:HALF].T
    phi = two_pi / 8 * ((r[None, :HALF] * b_hi[:, None]) % 8)
    sign = np.where(a % 2 == 0, 1.0, -1.0)[:, None]
    first = (ka[:HALF] == 0)[None]
    real = np.where(first, np.cos(phi) + sign * np.sin(phi), 2 * np.cos(th))
    imag = np.where(first, -np.sin(phi) + sign * np.cos(phi), -2 * np.sin(th))
    out = np.concatenate([real, imag], 1)
    source = ((-a) % 32) * 8
    flip0 = np.zeros((256, 256), np.float32)
    flip0[row, source + (-b_hi) % 8] = 1
    flip1 = np.zeros((256, 256), np.float32)
    flip1[row, source + (-b_hi - 1) % 8] = 1
    flip_lane = np.zeros((128, 128), np.float32)
    flip_lane[((-b_lo) % 4) * 32 + (-c) % 32, lane] = 1
    flips = np.concatenate([flip0, flip1], 0)
    small = np.concatenate([twiddle.reshape(2 * FULL, 128), flip_lane], 0)
    return np.concatenate([left, right, back, out], 0).astype(np.float32), flips, small.astype(np.float32)


def split(value):
    high = value.astype(BF16)
    return high, (value - high.astype(F32)).astype(BF16)


def mul3(left, right):
    dot = functools.partial(jnp.dot, preferred_element_type=F32)
    return dot(left[0], right[0]) + (dot(left[1], right[0]) + dot(left[0], right[1]))


def minmod(p, q):
    return jnp.maximum(jnp.minimum(p, q), jnp.minimum(jnp.maximum(p, q), 0.0))


def coords(vel):
    return vel // 8, (vel // 2) % 4, vel % 2


def partner(vel, off):
    y, x, core = coords(vel)
    return ((y + off[0]) % 2) * 8 + ((x + off[1]) % 4) * 2 + (core + off[2]) % 2


def step_kernel(
    spaces, layers,
    dist, kind, inflow_hbm, wall_hbm, gain_hbm, second_hbm, mats_hbm, flips_hbm, small_hbm,
    result,
    raw, inflow, wall, gain, second, mats, high, low, flips, small,
    ext, lane_sums, mass_row, mass_all, scales, read, cells, done, nat, weights, weights16, yh, yl,
    in_sem, mass_send, mass_recv, halo_send, halo_recv, go_send, go_recv, back_send, back_recv, own_sem,
):
    sp = lax.axis_index("space")
    me = lax.axis_index("vel")
    my_y, my_z = me // 4, me % 4
    chunks = layers // PAIR
    count = layers * 16

    loads = []
    for i, (source, target) in enumerate((
        (dist, raw), (wall_hbm, wall), (gain_hbm, gain), (second_hbm, second), (flips_hbm, flips),
        (small_hbm, small), (inflow_hbm, inflow), (mats_hbm, mats),
    )):
        loads.append(pltpu.make_async_copy(source, target, in_sem.at[i]))
        loads[-1].start()

    barrier = pltpu.get_barrier_semaphore()
    for off in ORDER:
        pl.semaphore_signal(barrier, inc=1, device_id=(sp, partner(me, off)), device_id_type=MESH)
    for near in (1, spaces - 1):
        pl.semaphore_signal(barrier, inc=1, device_id=(lax.rem(sp + near, spaces), me), device_id_type=MESH)

    sub = lax.broadcasted_iota(jnp.int32, (8, 128), 0)
    loads[1].wait()
    lane_sums[count:256, :] = jnp.zeros((256 - count, 128), F32)
    lane_sums[count:count + 1, :] = jnp.sum(wall[...], axis=0, keepdims=True)
    loads[0].wait()

    def sum_layer(x, _):
        pieces = []
        for y in range(4):
            block = raw[pl.ds(pl.multiple_of(256 * x + 64 * y, 64), 64), :].reshape(8, 8, 128)
            block = jnp.sum(block, axis=0)
            pieces.append(block + pltpu.roll(block, 4, 0))
        for i in range(2):
            lane_sums[pl.ds(pl.multiple_of(16 * x + 8 * i, 8), 8), :] = jnp.where(
                sub < 4, pieces[2 * i], pieces[2 * i + 1])
        return 0

    lax.fori_loop(0, layers, sum_layer, 0)
    mass_row[...] = jnp.sum(lane_sums[...].T, axis=0, keepdims=True)
    mass_all[me] = mass_row[...]

    pl.semaphore_wait(barrier, len(ORDER) + 2)

    sends = []
    for i, off in enumerate(ORDER):
        sends.append(pltpu.make_async_remote_copy(
            src_ref=mass_row, dst_ref=mass_all.at[me], send_sem=mass_send.at[i], recv_sem=mass_recv.at[i],
            device_id=(sp, partner(me, off)), device_id_type=MESH,
        ))
        sends[-1].start()

    lane = lax.broadcasted_iota(jnp.int32, (16, 128), 1) // 32
    for load in loads[2:]:
        load.wait()
    flip_lane = small[2 * FULL:, :]
    high[...], low[...] = split(mats[...])
    lane8 = lax.broadcasted_iota(jnp.int32, (8, 128), 1) // 32
    for t, (table, scale) in enumerate(((gain, 1.0 / NV), (second, COLLISION_AXIS / NV))):
        g = table[...]
        rev = jnp.dot(g, flip_lane, precision=HIGH, preferred_element_type=F32)
        mask = lax.broadcasted_iota(jnp.int32, (256, 128), 1) < 32
        rev0 = jnp.dot(flips[0:256, :], rev, precision=HIGH, preferred_element_type=F32)
        rev1 = jnp.dot(flips[256:512, :], rev, precision=HIGH, preferred_element_type=F32)
        rev = jnp.where(mask, rev0, rev1)
        nat[2 * t] = (0.5 * scale) * (g + rev)
        nat[2 * t + 1] = (0.5 * scale) * (g - rev)

    def order_weights(t, _):
        for r in range(8):
            upper, lower = r // 4, r % 4
            value = jnp.zeros((16, 128), F32)
            value16 = jnp.zeros((8, 128), F32)
            for q in range(4):
                rows = nat[t, pl.ds(2 * q + upper, 16, stride=8), :]
                row16 = jnp.broadcast_to(nat[t, pl.ds(128 + 2 * q + upper, 1), :], (8, 128))
                shift = (32 * (q - lower)) % 128
                if shift:
                    rows = pltpu.roll(rows, shift, 1)
                    row16 = pltpu.roll(row16, shift, 1)
                value = jnp.where(lane == q, rows, value)
                value16 = jnp.where(lane8 == q, row16, value16)
            weights[t, 16 * r:16 * r + 16, :] = value
            weights16[t, 8 * r:8 * r + 8, :] = jnp.where(sub == 0, value16, 0.0)
        return 0

    lax.fori_loop(0, 4, order_weights, 0)

    for copy in sends:
        copy.wait()
    total = jnp.sum(mass_all[...], axis=0)
    totals = jnp.broadcast_to(total, (128, 256)).T
    scales[...] = totals[:count] / totals[count:count + 1]

    def boundary_layer(x, _):
        for y in range(4):
            for z in range(4):
                what = jnp.full((8, 128), kind[y, z, x], jnp.int32)
                scale = jnp.broadcast_to(scales[pl.ds(x * 16 + 4 * y + z, 1), :], (8, 128))
                for e in range(2):
                    rows = slice(8 * e, 8 * e + 8)
                    value = raw[pl.ds(256 * x + 64 * y + 32 * e + z, 8, stride=4), :]
                    value = jnp.where(what == 1, scale * wall[rows, :], value)
                    ext[2 + x, y, z, rows, :] = jnp.where(what == 2, inflow[rows, :], value)
        return 0

    lax.fori_loop(0, 2, boundary_layer, 0)
    lax.fori_loop(layers - 2, layers, boundary_layer, 0)
    to_left = pltpu.make_async_remote_copy(
        src_ref=ext.at[pl.ds(2, 2)], dst_ref=ext.at[pl.ds(layers + 2, 2)],
        send_sem=halo_send.at[0], recv_sem=halo_recv.at[0],
        device_id=(lax.rem(sp + spaces - 1, spaces), me), device_id_type=MESH)
    to_right = pltpu.make_async_remote_copy(
        src_ref=ext.at[pl.ds(layers, 2)], dst_ref=ext.at[pl.ds(0, 2)],
        send_sem=halo_send.at[1], recv_sem=halo_recv.at[1],
        device_id=(lax.rem(sp + 1, spaces), me), device_id_type=MESH)

    @pl.when(sp > 0)
    def _():
        to_left.start()

    @pl.when(sp < spaces - 1)
    def _():
        to_right.start()

    @pl.when(sp == 0)
    def _():
        ext[0:2] = jnp.zeros((2, 4, 4, 16, 128), F32)

    @pl.when(sp == spaces - 1)
    def _():
        ext[layers + 2:layers + 4] = jnp.zeros((2, 4, 4, 16, 128), F32)

    lax.fori_loop(2, layers - 2, boundary_layer, 0)

    b_index = 4 * lax.broadcasted_iota(jnp.int32, (8, 128), 0) + lane8
    c_index = lax.broadcasted_iota(jnp.int32, (8, 128), 1) % 32

    def speed(index):
        return CFL * (2 * index - (VR - 1)).astype(F32) / (VR - 1)

    nu_y, nu_z = speed(b_index), speed(c_index)
    up_y, up_z = nu_y > 0, nu_z > 0
    size_y, size_z = jnp.abs(nu_y), jnp.abs(nu_z)
    coef_y = jnp.where(up_y, 0.5, -0.5) * (1.0 - size_y)
    coef_z = jnp.where(up_z, 0.5, -0.5) * (1.0 - size_z)

    def ring(s, coef, up, size):
        diff = [s[(i + 1) % 4] - s[i] for i in range(4)]
        face = [s[i] + coef * minmod(diff[i - 1], diff[i]) for i in range(4)]
        step = [face[(i + 1) % 4] - face[i] for i in range(4)]
        return [size * jnp.where(up, step[i - 1], -step[i]) for i in range(4)]

    def transport(x0):
        for e in range(2):
            rows = slice(8 * e, 8 * e + 8)
            nu_x = speed(jnp.full((8, 128), 2 * me + e, jnp.int32))
            up_x = nu_x > 0
            size_x = jnp.abs(nu_x)
            coef_x = jnp.where(up_x, 0.5, -0.5) * (1.0 - size_x)
            for y in range(4):
                for z in range(4):
                    s = [ext[x0 + i, y, z, rows, :] for i in range(6)]
                    diff = [s[i + 1] - s[i] for i in range(5)]
                    face = [s[i + 1] + coef_x * minmod(diff[i], diff[i + 1]) for i in range(4)]
                    step = [face[i + 1] - face[i] for i in range(3)]
                    for i in range(PAIR):
                        read[x0 + i, 4 * y + z, rows, :] = s[i + 2] - size_x * jnp.where(up_x, step[i], -step[i + 1])
            for i in range(PAIR):
                s = [[ext[x0 + 2 + i, y, z, rows, :] for z in range(4)] for y in range(4)]
                along_z = [ring(s[y], coef_z, up_z, size_z) for y in range(4)]
                along_y = [ring([s[y][z] for y in range(4)], coef_y, up_y, size_y) for z in range(4)]
                for y in range(4):
                    for z in range(4):
                        read[x0 + i, 4 * y + z, rows, :] -= along_z[y][z] + along_y[z][y]

    own = pl.ds(pl.multiple_of(16 * me, 16), 16)

    def send_chunk(k, x0):
        transport(x0)
        for i in range(PAIR):
            cells[x0 + i, own, :] = read[x0 + i, me]
        for off in ORDER:
            to = partner(me, off)
            pltpu.make_async_remote_copy(
                src_ref=read.at[pl.ds(x0, PAIR), to], dst_ref=cells.at[pl.ds(x0, PAIR), own, :],
                send_sem=go_send.at[k], recv_sem=go_recv.at[k],
                device_id=(sp, to), device_id_type=MESH,
            ).start()

    def first_of(k):
        return lax.rem(PAIR * k + 2, layers)

    def inner(k, _):
        send_chunk(k, first_of(k))
        return 0

    lax.fori_loop(0, chunks - 2, inner, 0)

    @pl.when(sp > 0)
    def _():
        to_right.wait_recv()

    @pl.when(sp < spaces - 1)
    def _():
        to_left.wait_recv()

    lax.fori_loop(chunks - 2, chunks, inner, 0)

    lh, ll = high.at[0:2 * FULL], low.at[0:2 * FULL]
    (rh, bh, oh), (rl, bl, ol) = (
        [ref.at[2 * FULL + 256 * i:2 * FULL + 256 * (i + 1)] for i in range(3)] for ref in (high, low))

    def collide(k, _):
        x0 = first_of(k)
        arrived = cells.at[pl.ds(x0, PAIR), pl.ds(0, 240), :]
        pltpu.make_async_copy(arrived, arrived, go_recv.at[k]).wait()
        field = jnp.concatenate([cells[x0], cells[x0 + 1]], 1)
        spec = mul3((lh[...], ll[...]), split(field))
        tc, ts = small[0:FULL, :], small[FULL:2 * FULL, :]
        parts = []
        for i in range(PAIR):
            re = spec[:FULL, 128 * i:128 * i + 128]
            im = spec[FULL:, 128 * i:128 * i + 128]
            parts.append(jnp.concatenate([re * tc + im * ts, im * tc - re * ts], 1))
        spec = mul3(split(jnp.concatenate(parts, 0)), (rh[...], rl[...]))
        tc, ts = small[0:HALF, :], small[FULL:FULL + HALF, :]
        for i in range(PAIR):
            re = spec[FULL * i:FULL * i + HALF, :128].reshape(8, 16, 128)
            im = spec[FULL * i:FULL * i + HALF, 128:].reshape(8, 16, 128)
            re16 = spec[FULL * i + HALF:FULL * (i + 1), :128]
            im16 = spec[FULL * i + HALF:FULL * (i + 1), 128:]
            for t in range(4):
                w = weights[t].reshape(8, 16, 128)
                for r in range(8):
                    w16 = weights16[t, 8 * r:8 * r + 8, :]
                    zr, zi = w[r] * re[r], w[r] * im[r]
                    zr = jnp.concatenate([zr[:8] - w16 * im16[r:r + 1, :], zr[8:]], 0)
                    zi = jnp.concatenate([zi[:8] + w16 * re16[r:r + 1, :], zi[8:]], 0)
                    if t % 2:
                        zr, zi = zi, -zr
                    rows = slice(HALF * (PAIR * t + i) + 16 * r, HALF * (PAIR * t + i) + 16 * r + 16)
                    yh[rows, :], yl[rows, :] = split(jnp.concatenate([zr, zi], 1))
        fields = []
        for t in range(4):
            rows = slice(PAIR * HALF * t, PAIR * HALF * (t + 1))
            value = mul3((yh[rows, :], yl[rows, :]), (bh[...], bl[...]))
            reals, imags = [], []
            for i in range(PAIR):
                re = value[HALF * i:HALF * (i + 1), :128]
                im = value[HALF * i:HALF * (i + 1), 128:]
                reals.append(re * tc - im * ts)
                imags.append(re * ts + im * tc)
            value = jnp.concatenate([jnp.concatenate(reals, 1), jnp.concatenate(imags, 1)], 0)
            fields.append(mul3((oh[...], ol[...]), split(value)))
        value = fields[0] * fields[2] - fields[1] * fields[3]
        for i in range(PAIR):
            done[x0 + i] = cells[x0 + i] + value[:, 128 * i:128 * i + 128]
        for off in ORDER:
            to = partner(me, off)
            pltpu.make_async_remote_copy(
                src_ref=done.at[pl.ds(x0, PAIR), pl.ds(pl.multiple_of(16 * to, 16), 16), :],
                dst_ref=result.at[pl.ds(x0, PAIR), my_y, my_z],
                send_sem=back_send.at[k], recv_sem=back_recv.at[k],
                device_id=(sp, to), device_id_type=MESH,
            ).start()
        return 0

    lax.fori_loop(0, chunks, collide, 0)

    mine = pltpu.make_async_copy(
        done.at[:, own, :], result.at[:, my_y, my_z], own_sem)
    mine.start()

    def finish(k, _):
        x0 = first_of(k)
        block = cells.at[pl.ds(x0, PAIR), pl.ds(0, 240), :]
        pltpu.make_async_copy(block, block, go_send.at[k]).wait()
        pltpu.make_async_copy(block, block, back_send.at[k]).wait()
        pltpu.make_async_copy(block, block, back_recv.at[k]).wait()
        return 0

    lax.fori_loop(0, chunks, finish, 0)
    mine.wait()

    @pl.when(sp > 0)
    def _():
        to_left.wait_send()

    @pl.when(sp < spaces - 1)
    def _():
        to_right.wait_send()


def place_kernel(layers, source, target, held, rows, in_sem, out_sem):
    step = layers // 4

    def load(i):
        return pltpu.make_async_copy(source.at[pl.ds(step * i, step)], held.at[pl.ds(step * i, step)], in_sem.at[i])

    def store(i):
        part = pl.ds(256 * step * i, 256 * step)
        return pltpu.make_async_copy(rows.at[part], target.at[part], out_sem.at[i])

    for i in range(4):
        load(i).start()
    for i in range(4):
        load(i).wait()

        def place(x, _):
            for y in range(4):
                for z in range(4):
                    for e in range(2):
                        rows[pl.ds(256 * x + 64 * y + 32 * e + z, 8, stride=4), :] = held[x, y, z, 8 * e:8 * e + 8, :]
            return 0

        lax.fori_loop(step * i, step * (i + 1), place, 0)
        store(i).start()
    for i in range(4):
        store(i).wait()


def shards(spaces, dist, cell_kind, inflow, wall_shape, gain_tables, second_tables):
    layers = dist.shape[0]
    mats, flips, small = tables()
    rows = dist.reshape(layers, 4, 4, 16, 128).transpose(0, 1, 3, 2, 4).reshape(layers * 256, 128)
    anywhere = pl.BlockSpec(memory_space=pl.ANY)
    chunks = layers // PAIR
    dma = pltpu.SemaphoreType.DMA
    result = pl.pallas_call(
        functools.partial(step_kernel, spaces, layers),
        out_shape=jax.ShapeDtypeStruct((layers, 4, 4, 16, 128), F32),
        in_specs=[anywhere, pl.BlockSpec(memory_space=pltpu.SMEM)] + [anywhere] * 7,
        out_specs=anywhere,
        scratch_shapes=[
            pltpu.VMEM((layers * 256, 128), F32),
            pltpu.VMEM((16, 128), F32), pltpu.VMEM((16, 128), F32),
            pltpu.VMEM((256, 128), F32), pltpu.VMEM((256, 128), F32),
            pltpu.VMEM(mats.shape, F32), pltpu.VMEM(mats.shape, BF16), pltpu.VMEM(mats.shape, BF16), pltpu.VMEM(flips.shape, F32), pltpu.VMEM(small.shape, F32),
            pltpu.VMEM((layers + 4, 4, 4, 16, 128), F32),
            pltpu.VMEM((256, 128), F32),
            pltpu.VMEM((1, 256), F32),
            pltpu.VMEM((16, 1, 256), F32),
            pltpu.VMEM((layers * 16, 128), F32),
            pltpu.VMEM((layers, 16, 16, 128), F32),
            pltpu.VMEM((layers, 256, 128), F32),
            pltpu.VMEM((layers, 256, 128), F32),
            pltpu.VMEM((4, 256, 128), F32),
            pltpu.VMEM((4, HALF, 128), F32),
            pltpu.VMEM((4, 64, 128), F32),
            pltpu.VMEM((4 * PAIR * HALF, 256), BF16),
            pltpu.VMEM((4 * PAIR * HALF, 256), BF16),
            dma((8,)),
            dma((15,)), dma((15,)),
            dma((2,)), dma((2,)),
            dma((chunks,)), dma((chunks,)),
            dma((chunks,)), dma((chunks,)),
            dma,
        ],
        compiler_params=pltpu.CompilerParams(
            collective_id=0, has_side_effects=True, vmem_limit_bytes=56 * 2**20),
    )(
        rows, cell_kind.transpose(1, 2, 0), inflow.reshape(16, 128), wall_shape.reshape(16, 128),
        gain_tables.reshape(256, 128), second_tables.reshape(256, 128),
        jnp.asarray(mats), jnp.asarray(flips), jnp.asarray(small),
    )
    placed = pl.pallas_call(
        functools.partial(place_kernel, layers),
        out_shape=jax.ShapeDtypeStruct((layers * 256, 128), F32),
        in_specs=[anywhere],
        out_specs=anywhere,
        scratch_shapes=[
            pltpu.VMEM((layers, 4, 4, 16, 128), F32), pltpu.VMEM((layers * 256, 128), F32), dma((4,)), dma((4,))],
        compiler_params=pltpu.CompilerParams(vmem_limit_bytes=56 * 2**20),
    )(result)
    return placed.reshape(layers, 4, 16, 4, 128).transpose(0, 1, 3, 2, 4).reshape(dist.shape)


def solution(mesh):
    placed = (P("space", None, None, "vel"), P("space", None, None), P("vel"), P("vel"), P(), P())
    return jax.shard_map(
        functools.partial(shards, mesh.shape["space"]),
        mesh=mesh, in_specs=placed, out_specs=P("space", None, None, "vel"), check_vma=False,
    )
```

```python
import functools
import math

import jax
import jax.numpy as jnp
import numpy as np
from jax import lax
from jax.experimental import pallas as pl
from jax.experimental.pallas import tpu as pltpu
from jax.sharding import PartitionSpec as P

VR = 32
NV = VR * VR * VR
CFL = 0.3
COLLISION_AXIS = 0.25
HIGH = lax.Precision.HIGHEST
MESH = pl.DeviceIdType.MESH
F32 = jnp.float32
BF16 = jnp.bfloat16

FULL = 136
HALF = 128
PAIR = 2

ORDER = (
    (1, 0, 0), (0, 1, 0), (0, 3, 1), (1, 2, 0), (1, 1, 0), (1, 3, 1), (0, 2, 0), (1, 0, 1),
    (0, 1, 1), (0, 3, 0), (1, 2, 1), (1, 1, 1), (1, 3, 0), (0, 2, 1), (0, 0, 1),
)


def tables():
    two_pi = 2.0 * math.pi
    row = np.arange(256)
    a, b_hi = row // 8, row % 8
    spec = np.arange(FULL)
    ka = np.where(spec < HALF, spec % 16, 16)
    r = np.where(spec < HALF, spec // 16, spec - HALF)
    theta = two_pi / 32 * ((ka[:, None] * a[None] + 4 * r[:, None] * b_hi[None]) % 32)
    left = np.concatenate([np.cos(theta), -np.sin(theta)], 0)
    lane = np.arange(128)
    b_lo, c = lane // 32, lane % 32
    angle = two_pi / 32 * ((8 * b_lo[:, None] * b_lo[None] + c[:, None] * c[None]) % 32)
    cos, sin = np.cos(angle), np.sin(angle)
    right = np.block([[cos, -sin], [sin, cos]])
    back = np.block([[cos, sin], [-sin, cos]])
    turn = two_pi / 32 * (r[:, None] * b_lo[None])
    twiddle = np.stack([np.cos(turn), np.sin(turn)])
    th = theta[:HALF].T
    phi = two_pi / 8 * ((r[None, :HALF] * b_hi[:, None]) % 8)
    sign = np.where(a % 2 == 0, 1.0, -1.0)[:, None]
    first = (ka[:HALF] == 0)[None]
    real = np.where(first, np.cos(phi) + sign * np.sin(phi), 2 * np.cos(th))
    imag = np.where(first, -np.sin(phi) + sign * np.cos(phi), -2 * np.sin(th))
    out = np.concatenate([real, imag], 1)
    source = ((-a) % 32) * 8
    flip0 = np.zeros((256, 256), np.float32)
    flip0[row, source + (-b_hi) % 8] = 1
    flip1 = np.zeros((256, 256), np.float32)
    flip1[row, source + (-b_hi - 1) % 8] = 1
    flip_lane = np.zeros((128, 128), np.float32)
    flip_lane[((-b_lo) % 4) * 32 + (-c) % 32, lane] = 1
    flips = np.concatenate([flip0, flip1], 0)
    small = np.concatenate([twiddle.reshape(2 * FULL, 128), flip_lane], 0)
    return np.concatenate([left, right, back, out], 0).astype(np.float32), flips, small.astype(np.float32)


def split(value):
    high = value.astype(BF16)
    return high, (value - high.astype(F32)).astype(BF16)


def mul3(left, right):
    dot = functools.partial(jnp.dot, preferred_element_type=F32)
    return dot(left[0], right[0]) + (dot(left[1], right[0]) + dot(left[0], right[1]))


def minmod(p, q):
    return jnp.maximum(jnp.minimum(p, q), jnp.minimum(jnp.maximum(p, q), 0.0))


def coords(vel):
    return vel // 8, (vel // 2) % 4, vel % 2


def partner(vel, off):
    y, x, core = coords(vel)
    return ((y + off[0]) % 2) * 8 + ((x + off[1]) % 4) * 2 + (core + off[2]) % 2


def step_kernel(
    spaces, layers,
    dist, kind, inflow_hbm, wall_hbm, gain_hbm, second_hbm, mats_hbm, flips_hbm, small_hbm,
    result,
    raw, inflow, wall, gain, second, mats, high, low, flips, small,
    ext, lane_sums, mass_row, mass_all, scales, read, cells, done, nat, weights, weights16, yh, yl,
    relay, in_sem, relay_sem, mass_send, mass_recv, halo_send, halo_recv, go_send, go_recv, back_send, back_recv, own_sem,
):
    sp = lax.axis_index("space")
    me = lax.axis_index("vel")
    my_y, my_z = me // 4, me % 4
    chunks = layers // PAIR
    count = layers * 16
    cross = spaces // 2

    loads = []
    for i, (source, target) in enumerate((
        (dist, raw), (wall_hbm, wall), (gain_hbm, gain), (second_hbm, second), (flips_hbm, flips),
        (small_hbm, small), (inflow_hbm, inflow), (mats_hbm, mats),
    )):
        loads.append(pltpu.make_async_copy(source, target, in_sem.at[i]))
        loads[-1].start()

    barrier = pltpu.get_barrier_semaphore()
    for off in ORDER:
        pl.semaphore_signal(barrier, inc=1, device_id=(sp, partner(me, off)), device_id_type=MESH)
    greeted = 0
    for other in range(spaces):
        ends = other in (cross - 1, cross)
        near = (sp == other - 1) | (sp == other + 1) | (sp == cross - 1) | (sp == cross)
        greet = (sp != other) if ends else near & (sp != other)
        greeted = greeted + jnp.where(greet, 1, 0)

        @pl.when(greet)
        def _():
            pl.semaphore_signal(barrier, inc=1, device_id=(other, me), device_id_type=MESH)

    sub = lax.broadcasted_iota(jnp.int32, (8, 128), 0)
    loads[1].wait()
    lane_sums[count:256, :] = jnp.zeros((256 - count, 128), F32)
    lane_sums[count:count + 1, :] = jnp.sum(wall[...], axis=0, keepdims=True)
    loads[0].wait()

    def sum_layer(x, _):
        pieces = []
        for y in range(4):
            block = raw[pl.ds(pl.multiple_of(256 * x + 64 * y, 64), 64), :].reshape(8, 8, 128)
            block = jnp.sum(block, axis=0)
            pieces.append(block + pltpu.roll(block, 4, 0))
        for i in range(2):
            lane_sums[pl.ds(pl.multiple_of(16 * x + 8 * i, 8), 8), :] = jnp.where(
                sub < 4, pieces[2 * i], pieces[2 * i + 1])
        return 0

    lax.fori_loop(0, layers, sum_layer, 0)
    mass_row[...] = jnp.sum(lane_sums[...].T, axis=0, keepdims=True)
    mass_all[me] = mass_row[...]

    pl.semaphore_wait(barrier, len(ORDER) + greeted)

    sends = []
    for i, off in enumerate(ORDER):
        sends.append(pltpu.make_async_remote_copy(
            src_ref=mass_row, dst_ref=mass_all.at[me], send_sem=mass_send.at[i], recv_sem=mass_recv.at[i],
            device_id=(sp, partner(me, off)), device_id_type=MESH,
        ))
        sends[-1].start()

    lane = lax.broadcasted_iota(jnp.int32, (16, 128), 1) // 32
    for load in loads[2:]:
        load.wait()
    flip_lane = small[2 * FULL:, :]
    high[...], low[...] = split(mats[...])
    lane8 = lax.broadcasted_iota(jnp.int32, (8, 128), 1) // 32
    for t, (table, scale) in enumerate(((gain, 1.0 / NV), (second, COLLISION_AXIS / NV))):
        g = table[...]
        rev = jnp.dot(g, flip_lane, precision=HIGH, preferred_element_type=F32)
        mask = lax.broadcasted_iota(jnp.int32, (256, 128), 1) < 32
        rev0 = jnp.dot(flips[0:256, :], rev, precision=HIGH, preferred_element_type=F32)
        rev1 = jnp.dot(flips[256:512, :], rev, precision=HIGH, preferred_element_type=F32)
        rev = jnp.where(mask, rev0, rev1)
        nat[2 * t] = (0.5 * scale) * (g + rev)
        nat[2 * t + 1] = (0.5 * scale) * (g - rev)

    def order_weights(t, _):
        for r in range(8):
            upper, lower = r // 4, r % 4
            value = jnp.zeros((16, 128), F32)
            value16 = jnp.zeros((8, 128), F32)
            for q in range(4):
                rows = nat[t, pl.ds(2 * q + upper, 16, stride=8), :]
                row16 = jnp.broadcast_to(nat[t, pl.ds(128 + 2 * q + upper, 1), :], (8, 128))
                shift = (32 * (q - lower)) % 128
                if shift:
                    rows = pltpu.roll(rows, shift, 1)
                    row16 = pltpu.roll(row16, shift, 1)
                value = jnp.where(lane == q, rows, value)
                value16 = jnp.where(lane8 == q, row16, value16)
            weights[t, 16 * r:16 * r + 16, :] = value
            weights16[t, 8 * r:8 * r + 8, :] = jnp.where(sub == 0, value16, 0.0)
        return 0

    lax.fori_loop(0, 4, order_weights, 0)

    for copy in sends:
        copy.wait_recv()
    total = jnp.sum(mass_all[...], axis=0)
    totals = jnp.broadcast_to(total, (128, 256)).T
    scales[...] = totals[:count] / totals[count:count + 1]

    def boundary_layer(x, _):
        for y in range(4):
            for z in range(4):
                what = jnp.full((8, 128), kind[y, z, x], jnp.int32)
                scale = jnp.broadcast_to(scales[pl.ds(x * 16 + 4 * y + z, 1), :], (8, 128))
                for e in range(2):
                    rows = slice(8 * e, 8 * e + 8)
                    value = raw[pl.ds(256 * x + 64 * y + 32 * e + z, 8, stride=4), :]
                    value = jnp.where(what == 1, scale * wall[rows, :], value)
                    ext[2 + x, y, z, rows, :] = jnp.where(what == 2, inflow[rows, :], value)
        return 0

    lax.fori_loop(0, 2, boundary_layer, 0)
    lax.fori_loop(layers - 2, layers, boundary_layer, 0)
    to_left = pltpu.make_async_remote_copy(
        src_ref=ext.at[pl.ds(2, 2)], dst_ref=ext.at[pl.ds(layers + 2, 2)],
        send_sem=halo_send.at[0], recv_sem=halo_recv.at[0],
        device_id=(lax.rem(sp + spaces - 1, spaces), me), device_id_type=MESH)
    to_right = pltpu.make_async_remote_copy(
        src_ref=ext.at[pl.ds(layers, 2)], dst_ref=ext.at[pl.ds(0, 2)],
        send_sem=halo_send.at[1], recv_sem=halo_recv.at[1],
        device_id=(lax.rem(sp + 1, spaces), me), device_id_type=MESH)

    def piece(x, p):
        return ext.at[pl.ds(x, 2), p // 2, pl.ds(2 * (p % 2), 2)]

    @pl.when((sp > 0) & (sp != cross))
    def _():
        to_left.start()

    @pl.when((sp < spaces - 1) & (sp != cross - 1))
    def _():
        to_right.start()

    @pl.when(sp == cross - 1)
    def _():
        for p in range(cross):
            pltpu.make_async_remote_copy(
                src_ref=piece(layers, p), dst_ref=piece(0, p) if p == 0 else relay,
                send_sem=halo_send.at[1], recv_sem=halo_recv.at[1] if p == 0 else relay_sem.at[0],
                device_id=(cross + p, me), device_id_type=MESH).start()

    @pl.when(sp == cross)
    def _():
        for p in range(cross):
            pltpu.make_async_remote_copy(
                src_ref=piece(2, p), dst_ref=piece(layers + 2, p) if p == cross - 1 else relay,
                send_sem=halo_send.at[0], recv_sem=halo_recv.at[0] if p == cross - 1 else relay_sem.at[0],
                device_id=(p, me), device_id_type=MESH).start()

    up = lax.rem(sp, cross)
    relay_right = pltpu.make_async_remote_copy(
        src_ref=relay, dst_ref=piece(0, up), send_sem=relay_sem.at[1], recv_sem=halo_recv.at[1],
        device_id=(cross, me), device_id_type=MESH)
    relay_left = pltpu.make_async_remote_copy(
        src_ref=relay, dst_ref=piece(layers + 2, up), send_sem=relay_sem.at[1], recv_sem=halo_recv.at[0],
        device_id=(cross - 1, me), device_id_type=MESH)

    @pl.when(sp == 0)
    def _():
        ext[0:2] = jnp.zeros((2, 4, 4, 16, 128), F32)

    @pl.when(sp == spaces - 1)
    def _():
        ext[layers + 2:layers + 4] = jnp.zeros((2, 4, 4, 16, 128), F32)

    lax.fori_loop(2, layers - 2, boundary_layer, 0)

    b_index = 4 * lax.broadcasted_iota(jnp.int32, (8, 128), 0) + lane8
    c_index = lax.broadcasted_iota(jnp.int32, (8, 128), 1) % 32

    def speed(index):
        return CFL * (2 * index - (VR - 1)).astype(F32) / (VR - 1)

    nu_y, nu_z = speed(b_index), speed(c_index)
    up_y, up_z = nu_y > 0, nu_z > 0
    size_y, size_z = jnp.abs(nu_y), jnp.abs(nu_z)
    coef_y = jnp.where(up_y, 0.5, -0.5) * (1.0 - size_y)
    coef_z = jnp.where(up_z, 0.5, -0.5) * (1.0 - size_z)

    def ring(s, coef, up, size):
        diff = [s[(i + 1) % 4] - s[i] for i in range(4)]
        face = [s[i] + coef * minmod(diff[i - 1], diff[i]) for i in range(4)]
        step = [face[(i + 1) % 4] - face[i] for i in range(4)]
        return [size * jnp.where(up, step[i - 1], -step[i]) for i in range(4)]

    def transport(x0):
        for e in range(2):
            rows = slice(8 * e, 8 * e + 8)
            nu_x = speed(jnp.full((8, 128), 2 * me + e, jnp.int32))
            up_x = nu_x > 0
            size_x = jnp.abs(nu_x)
            coef_x = jnp.where(up_x, 0.5, -0.5) * (1.0 - size_x)
            for y in range(4):
                for z in range(4):
                    s = [ext[x0 + i, y, z, rows, :] for i in range(6)]
                    diff = [s[i + 1] - s[i] for i in range(5)]
                    face = [s[i + 1] + coef_x * minmod(diff[i], diff[i + 1]) for i in range(4)]
                    step = [face[i + 1] - face[i] for i in range(3)]
                    for i in range(PAIR):
                        read[x0 + i, 4 * y + z, rows, :] = s[i + 2] - size_x * jnp.where(up_x, step[i], -step[i + 1])
            for i in range(PAIR):
                s = [[ext[x0 + 2 + i, y, z, rows, :] for z in range(4)] for y in range(4)]
                along_z = [ring(s[y], coef_z, up_z, size_z) for y in range(4)]
                along_y = [ring([s[y][z] for y in range(4)], coef_y, up_y, size_y) for z in range(4)]
                for y in range(4):
                    for z in range(4):
                        read[x0 + i, 4 * y + z, rows, :] -= along_z[y][z] + along_y[z][y]

    own = pl.ds(pl.multiple_of(16 * me, 16), 16)

    def send_chunk(k, x0):
        transport(x0)
        for i in range(PAIR):
            cells[x0 + i, own, :] = read[x0 + i, me]
        for off in ORDER:
            to = partner(me, off)
            pltpu.make_async_remote_copy(
                src_ref=read.at[pl.ds(x0, PAIR), to], dst_ref=cells.at[pl.ds(x0, PAIR), own, :],
                send_sem=go_send.at[k], recv_sem=go_recv.at[k],
                device_id=(sp, to), device_id_type=MESH,
            ).start()

    def first_of(k):
        return lax.rem(PAIR * k + 2, layers)

    def inner(k, _):
        send_chunk(k, first_of(k))
        return 0

    lax.fori_loop(0, 2, inner, 0)

    @pl.when(sp > cross)
    def _():
        pltpu.make_async_copy(relay, relay, relay_sem.at[0]).wait()
        relay_right.start()

    @pl.when(sp < cross - 1)
    def _():
        pltpu.make_async_copy(relay, relay, relay_sem.at[0]).wait()
        relay_left.start()

    lax.fori_loop(2, chunks - 2, inner, 0)

    @pl.when(sp > 0)
    def _():
        to_right.wait_recv()

    @pl.when(sp < spaces - 1)
    def _():
        to_left.wait_recv()

    lax.fori_loop(chunks - 2, chunks, inner, 0)

    lh, ll = high.at[0:2 * FULL], low.at[0:2 * FULL]
    (rh, bh, oh), (rl, bl, ol) = (
        [ref.at[2 * FULL + 256 * i:2 * FULL + 256 * (i + 1)] for i in range(3)] for ref in (high, low))

    def collide(k, _):
        x0 = first_of(k)
        arrived = cells.at[pl.ds(x0, PAIR), pl.ds(0, 240), :]
        pltpu.make_async_copy(arrived, arrived, go_recv.at[k]).wait()
        field = jnp.concatenate([cells[x0], cells[x0 + 1]], 1)
        spec = mul3((lh[...], ll[...]), split(field))
        tc, ts = small[0:FULL, :], small[FULL:2 * FULL, :]
        parts = []
        for i in range(PAIR):
            re = spec[:FULL, 128 * i:128 * i + 128]
            im = spec[FULL:, 128 * i:128 * i + 128]
            parts.append(jnp.concatenate([re * tc + im * ts, im * tc - re * ts], 1))
        spec = mul3(split(jnp.concatenate(parts, 0)), (rh[...], rl[...]))
        tc, ts = small[0:HALF, :], small[FULL:FULL + HALF, :]
        for i in range(PAIR):
            re = spec[FULL * i:FULL * i + HALF, :128].reshape(8, 16, 128)
            im = spec[FULL * i:FULL * i + HALF, 128:].reshape(8, 16, 128)
            re16 = spec[FULL * i + HALF:FULL * (i + 1), :128]
            im16 = spec[FULL * i + HALF:FULL * (i + 1), 128:]
            for t in range(4):
                w = weights[t].reshape(8, 16, 128)
                for r in range(8):
                    w16 = weights16[t, 8 * r:8 * r + 8, :]
                    zr, zi = w[r] * re[r], w[r] * im[r]
                    zr = jnp.concatenate([zr[:8] - w16 * im16[r:r + 1, :], zr[8:]], 0)
                    zi = jnp.concatenate([zi[:8] + w16 * re16[r:r + 1, :], zi[8:]], 0)
                    if t % 2:
                        zr, zi = zi, -zr
                    rows = slice(HALF * (PAIR * t + i) + 16 * r, HALF * (PAIR * t + i) + 16 * r + 16)
                    yh[rows, :], yl[rows, :] = split(jnp.concatenate([zr, zi], 1))
        fields = []
        for t in range(4):
            rows = slice(PAIR * HALF * t, PAIR * HALF * (t + 1))
            value = mul3((yh[rows, :], yl[rows, :]), (bh[...], bl[...]))
            reals, imags = [], []
            for i in range(PAIR):
                re = value[HALF * i:HALF * (i + 1), :128]
                im = value[HALF * i:HALF * (i + 1), 128:]
                reals.append(re * tc - im * ts)
                imags.append(re * ts + im * tc)
            value = jnp.concatenate([jnp.concatenate(reals, 1), jnp.concatenate(imags, 1)], 0)
            fields.append(mul3((oh[...], ol[...]), split(value)))
        value = fields[0] * fields[2] - fields[1] * fields[3]
        for i in range(PAIR):
            done[x0 + i] = cells[x0 + i] + value[:, 128 * i:128 * i + 128]
        for off in ORDER:
            to = partner(me, off)
            pltpu.make_async_remote_copy(
                src_ref=done.at[pl.ds(x0, PAIR), pl.ds(pl.multiple_of(16 * to, 16), 16), :],
                dst_ref=result.at[pl.ds(x0, PAIR), my_y, my_z],
                send_sem=back_send.at[k], recv_sem=back_recv.at[k],
                device_id=(sp, to), device_id_type=MESH,
            ).start()
        return 0

    lax.fori_loop(0, chunks, collide, 0)

    mine = pltpu.make_async_copy(
        done.at[:, own, :], result.at[:, my_y, my_z], own_sem)
    mine.start()

    def finish(k, _):
        x0 = first_of(k)
        block = cells.at[pl.ds(x0, PAIR), pl.ds(0, 240), :]
        pltpu.make_async_copy(block, block, go_send.at[k]).wait()
        pltpu.make_async_copy(block, block, back_send.at[k]).wait()
        pltpu.make_async_copy(block, block, back_recv.at[k]).wait()
        return 0

    lax.fori_loop(0, chunks, finish, 0)
    mine.wait()

    @pl.when(sp > 0)
    def _():
        to_left.wait_send()

    @pl.when(sp < spaces - 1)
    def _():
        to_right.wait_send()

    @pl.when(sp > cross)
    def _():
        relay_right.wait_send()

    @pl.when(sp < cross - 1)
    def _():
        relay_left.wait_send()

    for copy in sends:
        copy.wait_send()


def place_kernel(layers, source, target, held, rows, in_sem, out_sem):
    step = layers // 4

    def load(i):
        return pltpu.make_async_copy(source.at[pl.ds(step * i, step)], held.at[pl.ds(step * i, step)], in_sem.at[i])

    def store(i):
        part = pl.ds(256 * step * i, 256 * step)
        return pltpu.make_async_copy(rows.at[part], target.at[part], out_sem.at[i])

    for i in range(4):
        load(i).start()
    for i in range(4):
        load(i).wait()

        def place(x, _):
            for y in range(4):
                for z in range(4):
                    for e in range(2):
                        rows[pl.ds(256 * x + 64 * y + 32 * e + z, 8, stride=4), :] = held[x, y, z, 8 * e:8 * e + 8, :]
            return 0

        lax.fori_loop(step * i, step * (i + 1), place, 0)
        store(i).start()
    for i in range(4):
        store(i).wait()


def shards(spaces, dist, cell_kind, inflow, wall_shape, gain_tables, second_tables):
    layers = dist.shape[0]
    mats, flips, small = tables()
    rows = dist.reshape(layers, 4, 4, 16, 128).transpose(0, 1, 3, 2, 4).reshape(layers * 256, 128)
    anywhere = pl.BlockSpec(memory_space=pl.ANY)
    chunks = layers // PAIR
    dma = pltpu.SemaphoreType.DMA
    result = pl.pallas_call(
        functools.partial(step_kernel, spaces, layers),
        out_shape=jax.ShapeDtypeStruct((layers, 4, 4, 16, 128), F32),
        in_specs=[anywhere, pl.BlockSpec(memory_space=pltpu.SMEM)] + [anywhere] * 7,
        out_specs=anywhere,
        scratch_shapes=[
            pltpu.VMEM((layers * 256, 128), F32),
            pltpu.VMEM((16, 128), F32), pltpu.VMEM((16, 128), F32),
            pltpu.VMEM((256, 128), F32), pltpu.VMEM((256, 128), F32),
            pltpu.VMEM(mats.shape, F32), pltpu.VMEM(mats.shape, BF16), pltpu.VMEM(mats.shape, BF16), pltpu.VMEM(flips.shape, F32), pltpu.VMEM(small.shape, F32),
            pltpu.VMEM((layers + 4, 4, 4, 16, 128), F32),
            pltpu.VMEM((256, 128), F32),
            pltpu.VMEM((1, 256), F32),
            pltpu.VMEM((16, 1, 256), F32),
            pltpu.VMEM((layers * 16, 128), F32),
            pltpu.VMEM((layers, 16, 16, 128), F32),
            pltpu.VMEM((layers, 256, 128), F32),
            pltpu.VMEM((layers, 256, 128), F32),
            pltpu.VMEM((4, 256, 128), F32),
            pltpu.VMEM((4, HALF, 128), F32),
            pltpu.VMEM((4, 64, 128), F32),
            pltpu.VMEM((4 * PAIR * HALF, 256), BF16),
            pltpu.VMEM((4 * PAIR * HALF, 256), BF16),
            pltpu.VMEM((2, 2, 16, 128), F32),
            dma((8,)), dma((2,)),
            dma((15,)), dma((15,)),
            dma((2,)), dma((2,)),
            dma((chunks,)), dma((chunks,)),
            dma((chunks,)), dma((chunks,)),
            dma,
        ],
        compiler_params=pltpu.CompilerParams(
            collective_id=0, has_side_effects=True, vmem_limit_bytes=56 * 2**20),
    )(
        rows, cell_kind.transpose(1, 2, 0), inflow.reshape(16, 128), wall_shape.reshape(16, 128),
        gain_tables.reshape(256, 128), second_tables.reshape(256, 128),
        jnp.asarray(mats), jnp.asarray(flips), jnp.asarray(small),
    )
    placed = pl.pallas_call(
        functools.partial(place_kernel, layers),
        out_shape=jax.ShapeDtypeStruct((layers * 256, 128), F32),
        in_specs=[anywhere],
        out_specs=anywhere,
        scratch_shapes=[
            pltpu.VMEM((layers, 4, 4, 16, 128), F32), pltpu.VMEM((layers * 256, 128), F32), dma((4,)), dma((4,))],
        compiler_params=pltpu.CompilerParams(vmem_limit_bytes=56 * 2**20),
    )(result)
    return placed.reshape(layers, 4, 16, 4, 128).transpose(0, 1, 3, 2, 4).reshape(dist.shape)


def solution(mesh):
    placed = (P("space", None, None, "vel"), P("space", None, None), P("vel"), P("vel"), P(), P())
    return jax.shard_map(
        functools.partial(shards, mesh.shape["space"]),
        mesh=mesh, in_specs=placed, out_specs=P("space", None, None, "vel"), check_vma=False,
    )
```

```python
import functools
import math

import jax
import jax.numpy as jnp
import numpy as np
from jax import lax
from jax.experimental import pallas as pl
from jax.experimental.pallas import tpu as pltpu
from jax.sharding import PartitionSpec as P

VR = 32
NV = VR * VR * VR
CFL = 0.3
COLLISION_AXIS = 0.25
HIGH = lax.Precision.HIGHEST
MESH = pl.DeviceIdType.MESH
F32 = jnp.float32
BF16 = jnp.bfloat16

FULL = 136
HALF = 128
PAIR = 2

ORDER = (
    (1, 0, 0), (0, 1, 0), (0, 3, 1), (1, 2, 0), (1, 1, 0), (1, 3, 1), (0, 2, 0), (1, 0, 1),
    (0, 1, 1), (0, 3, 0), (1, 2, 1), (1, 1, 1), (1, 3, 0), (0, 2, 1), (0, 0, 1),
)


def tables():
    two_pi = 2.0 * math.pi
    row = np.arange(256)
    a, b_hi = row // 8, row % 8
    spec = np.arange(FULL)
    ka = np.where(spec < HALF, spec % 16, 16)
    r = np.where(spec < HALF, spec // 16, spec - HALF)
    theta = two_pi / 32 * ((ka[:, None] * a[None] + 4 * r[:, None] * b_hi[None]) % 32)
    left = np.concatenate([np.cos(theta), -np.sin(theta)], 0)
    lane = np.arange(128)
    b_lo, c = lane // 32, lane % 32
    angle = two_pi / 32 * ((8 * b_lo[:, None] * b_lo[None] + c[:, None] * c[None]) % 32)
    cos, sin = np.cos(angle), np.sin(angle)
    right = np.block([[cos, -sin], [sin, cos]])
    back = np.block([[cos, sin], [-sin, cos]])
    turn = two_pi / 32 * (r[:, None] * b_lo[None])
    twiddle = np.stack([np.cos(turn), np.sin(turn)])
    th = theta[:HALF].T
    phi = two_pi / 8 * ((r[None, :HALF] * b_hi[:, None]) % 8)
    sign = np.where(a % 2 == 0, 1.0, -1.0)[:, None]
    first = (ka[:HALF] == 0)[None]
    real = np.where(first, np.cos(phi) + sign * np.sin(phi), 2 * np.cos(th))
    imag = np.where(first, -np.sin(phi) + sign * np.cos(phi), -2 * np.sin(th))
    out = np.concatenate([real, imag], 1)
    source = ((-a) % 32) * 8
    flip0 = np.zeros((256, 256), np.float32)
    flip0[row, source + (-b_hi) % 8] = 1
    flip1 = np.zeros((256, 256), np.float32)
    flip1[row, source + (-b_hi - 1) % 8] = 1
    flip_lane = np.zeros((128, 128), np.float32)
    flip_lane[((-b_lo) % 4) * 32 + (-c) % 32, lane] = 1
    flips = np.concatenate([flip0, flip1], 0)
    small = np.concatenate([twiddle.reshape(2 * FULL, 128), flip_lane], 0)
    return np.concatenate([left, right, back, out], 0).astype(np.float32), flips, small.astype(np.float32)


def split(value):
    high = value.astype(BF16)
    return high, (value - high.astype(F32)).astype(BF16)


def mul3(left, right):
    dot = functools.partial(jnp.dot, preferred_element_type=F32)
    return dot(left[0], right[0]) + (dot(left[1], right[0]) + dot(left[0], right[1]))


def minmod(p, q):
    return jnp.maximum(jnp.minimum(p, q), jnp.minimum(jnp.maximum(p, q), 0.0))


def coords(vel):
    return vel // 8, (vel // 2) % 4, vel % 2


def partner(vel, off):
    y, x, core = coords(vel)
    return ((y + off[0]) % 2) * 8 + ((x + off[1]) % 4) * 2 + (core + off[2]) % 2


def step_kernel(
    spaces, layers,
    dist, kind, inflow_hbm, wall_hbm, gain_hbm, second_hbm, mats_hbm, flips_hbm, small_hbm,
    result,
    raw, inflow, wall, gain, second, mats, high, low, flips, small,
    ext, lane_sums, mass_row, mass_all, scales, read, cells, done, nat, weights, weights16, yh, yl,
    relay, in_sem, relay_sem, mass_send, mass_recv, halo_send, halo_recv, go_send, go_recv, back_send, back_recv, own_sem,
):
    sp = lax.axis_index("space")
    me = lax.axis_index("vel")
    my_y, my_z = me // 4, me % 4
    chunks = layers // PAIR
    count = layers * 16
    cross = spaces // 2

    loads = []
    for i, (source, target) in enumerate((
        (dist, raw), (wall_hbm, wall), (gain_hbm, gain), (second_hbm, second), (flips_hbm, flips),
        (small_hbm, small), (mats_hbm, mats), (inflow_hbm, inflow),
    )):
        loads.append(pltpu.make_async_copy(source, target, in_sem.at[i]))
        loads[-1].start()

    barrier = pltpu.get_barrier_semaphore()
    for off in ORDER:
        pl.semaphore_signal(barrier, inc=1, device_id=(sp, partner(me, off)), device_id_type=MESH)
    greeted = 0
    for other in range(spaces):
        ends = other in (cross - 1, cross)
        near = (sp == other - 1) | (sp == other + 1) | (sp == cross - 1) | (sp == cross)
        greet = (sp != other) if ends else near & (sp != other)
        greeted = greeted + jnp.where(greet, 1, 0)

        @pl.when(greet)
        def _():
            pl.semaphore_signal(barrier, inc=1, device_id=(other, me), device_id_type=MESH)

    sub = lax.broadcasted_iota(jnp.int32, (8, 128), 0)
    loads[1].wait()
    lane_sums[count:256, :] = jnp.zeros((256 - count, 128), F32)
    lane_sums[count:count + 1, :] = jnp.sum(wall[...], axis=0, keepdims=True)
    loads[0].wait()

    def sum_layer(x, _):
        pieces = []
        for y in range(4):
            block = raw[pl.ds(pl.multiple_of(256 * x + 64 * y, 64), 64), :].reshape(8, 8, 128)
            block = jnp.sum(block, axis=0)
            pieces.append(block + pltpu.roll(block, 4, 0))
        for i in range(2):
            lane_sums[pl.ds(pl.multiple_of(16 * x + 8 * i, 8), 8), :] = jnp.where(
                sub < 4, pieces[2 * i], pieces[2 * i + 1])
        return 0

    lax.fori_loop(0, layers, sum_layer, 0)
    mass_row[...] = jnp.sum(lane_sums[...].T, axis=0, keepdims=True)
    mass_all[me] = mass_row[...]

    pl.semaphore_wait(barrier, len(ORDER) + greeted)

    sends = []
    for i, off in enumerate(ORDER):
        sends.append(pltpu.make_async_remote_copy(
            src_ref=mass_row, dst_ref=mass_all.at[me], send_sem=mass_send.at[i], recv_sem=mass_recv.at[i],
            device_id=(sp, partner(me, off)), device_id_type=MESH,
        ))
        sends[-1].start()

    lane = lax.broadcasted_iota(jnp.int32, (16, 128), 1) // 32
    lane8 = lax.broadcasted_iota(jnp.int32, (8, 128), 1) // 32

    def prepare():
        for load in loads[2:-1]:
            load.wait()
        flip_lane = small[2 * FULL:, :]
        high[...], low[...] = split(mats[...])
        for t, (table, scale) in enumerate(((gain, 1.0 / NV), (second, COLLISION_AXIS / NV))):
            g = table[...]
            rev = jnp.dot(g, flip_lane, precision=HIGH, preferred_element_type=F32)
            mask = lax.broadcasted_iota(jnp.int32, (256, 128), 1) < 32
            rev0 = jnp.dot(flips[0:256, :], rev, precision=HIGH, preferred_element_type=F32)
            rev1 = jnp.dot(flips[256:512, :], rev, precision=HIGH, preferred_element_type=F32)
            rev = jnp.where(mask, rev0, rev1)
            nat[2 * t] = (0.5 * scale) * (g + rev)
            nat[2 * t + 1] = (0.5 * scale) * (g - rev)

        def order_weights(t, _):
            for r in range(8):
                upper, lower = r // 4, r % 4
                value = jnp.zeros((16, 128), F32)
                value16 = jnp.zeros((8, 128), F32)
                for q in range(4):
                    rows = nat[t, pl.ds(2 * q + upper, 16, stride=8), :]
                    row16 = jnp.broadcast_to(nat[t, pl.ds(128 + 2 * q + upper, 1), :], (8, 128))
                    shift = (32 * (q - lower)) % 128
                    if shift:
                        rows = pltpu.roll(rows, shift, 1)
                        row16 = pltpu.roll(row16, shift, 1)
                    value = jnp.where(lane == q, rows, value)
                    value16 = jnp.where(lane8 == q, row16, value16)
                weights[t, 16 * r:16 * r + 16, :] = value
                weights16[t, 8 * r:8 * r + 8, :] = jnp.where(sub == 0, value16, 0.0)
            return 0

        lax.fori_loop(0, 4, order_weights, 0)

    loads[-1].wait()
    for copy in sends:
        copy.wait_recv()
    total = jnp.sum(mass_all[...], axis=0)
    totals = jnp.broadcast_to(total, (128, 256)).T
    scales[...] = totals[:count] / totals[count:count + 1]

    def boundary_layer(x, _):
        for y in range(4):
            for z in range(4):
                what = jnp.full((8, 128), kind[y, z, x], jnp.int32)
                scale = jnp.broadcast_to(scales[pl.ds(x * 16 + 4 * y + z, 1), :], (8, 128))
                for e in range(2):
                    rows = slice(8 * e, 8 * e + 8)
                    value = raw[pl.ds(256 * x + 64 * y + 32 * e + z, 8, stride=4), :]
                    value = jnp.where(what == 1, scale * wall[rows, :], value)
                    ext[2 + x, y, z, rows, :] = jnp.where(what == 2, inflow[rows, :], value)
        return 0

    to_left = pltpu.make_async_remote_copy(
        src_ref=ext.at[pl.ds(2, 2)], dst_ref=ext.at[pl.ds(layers + 2, 2)],
        send_sem=halo_send.at[0], recv_sem=halo_recv.at[0],
        device_id=(lax.rem(sp + spaces - 1, spaces), me), device_id_type=MESH)
    to_right = pltpu.make_async_remote_copy(
        src_ref=ext.at[pl.ds(layers, 2)], dst_ref=ext.at[pl.ds(0, 2)],
        send_sem=halo_send.at[1], recv_sem=halo_recv.at[1],
        device_id=(lax.rem(sp + 1, spaces), me), device_id_type=MESH)

    def piece(x, p):
        return ext.at[pl.ds(x, 2), p // 2, pl.ds(2 * (p % 2), 2)]

    up = lax.rem(sp, cross)
    relay_right = pltpu.make_async_remote_copy(
        src_ref=relay, dst_ref=piece(0, up), send_sem=relay_sem.at[1], recv_sem=halo_recv.at[1],
        device_id=(cross, me), device_id_type=MESH)
    relay_left = pltpu.make_async_remote_copy(
        src_ref=relay, dst_ref=piece(layers + 2, up), send_sem=relay_sem.at[1], recv_sem=halo_recv.at[0],
        device_id=(cross - 1, me), device_id_type=MESH)

    @pl.when(sp == 0)
    def _():
        ext[0:2] = jnp.zeros((2, 4, 4, 16, 128), F32)

    @pl.when(sp == spaces - 1)
    def _():
        ext[layers + 2:layers + 4] = jnp.zeros((2, 4, 4, 16, 128), F32)


    b_index = 4 * lax.broadcasted_iota(jnp.int32, (8, 128), 0) + lane8
    c_index = lax.broadcasted_iota(jnp.int32, (8, 128), 1) % 32

    def speed(index):
        return CFL * (2 * index - (VR - 1)).astype(F32) / (VR - 1)

    nu_y, nu_z = speed(b_index), speed(c_index)
    up_y, up_z = nu_y > 0, nu_z > 0
    size_y, size_z = jnp.abs(nu_y), jnp.abs(nu_z)
    coef_y = jnp.where(up_y, 0.5, -0.5) * (1.0 - size_y)
    coef_z = jnp.where(up_z, 0.5, -0.5) * (1.0 - size_z)

    def ring(s, coef, up, size):
        diff = [s[(i + 1) % 4] - s[i] for i in range(4)]
        face = [s[i] + coef * minmod(diff[i - 1], diff[i]) for i in range(4)]
        step = [face[(i + 1) % 4] - face[i] for i in range(4)]
        return [size * jnp.where(up, step[i - 1], -step[i]) for i in range(4)]

    def transport(x0):
        for e in range(2):
            rows = slice(8 * e, 8 * e + 8)
            nu_x = speed(jnp.full((8, 128), 2 * me + e, jnp.int32))
            up_x = nu_x > 0
            size_x = jnp.abs(nu_x)
            coef_x = jnp.where(up_x, 0.5, -0.5) * (1.0 - size_x)
            for y in range(4):
                for z in range(4):
                    s = [ext[x0 + i, y, z, rows, :] for i in range(6)]
                    diff = [s[i + 1] - s[i] for i in range(5)]
                    face = [s[i + 1] + coef_x * minmod(diff[i], diff[i + 1]) for i in range(4)]
                    step = [face[i + 1] - face[i] for i in range(3)]
                    for i in range(PAIR):
                        read[x0 + i, 4 * y + z, rows, :] = s[i + 2] - size_x * jnp.where(up_x, step[i], -step[i + 1])
            for i in range(PAIR):
                s = [[ext[x0 + 2 + i, y, z, rows, :] for z in range(4)] for y in range(4)]
                along_z = [ring(s[y], coef_z, up_z, size_z) for y in range(4)]
                along_y = [ring([s[y][z] for y in range(4)], coef_y, up_y, size_y) for z in range(4)]
                for y in range(4):
                    for z in range(4):
                        read[x0 + i, 4 * y + z, rows, :] -= along_z[y][z] + along_y[z][y]

    own = pl.ds(pl.multiple_of(16 * me, 16), 16)

    def send_chunk(k, x0):
        transport(x0)
        for i in range(PAIR):
            cells[x0 + i, own, :] = read[x0 + i, me]
        for off in ORDER:
            to = partner(me, off)
            pltpu.make_async_remote_copy(
                src_ref=read.at[pl.ds(x0, PAIR), to], dst_ref=cells.at[pl.ds(x0, PAIR), own, :],
                send_sem=go_send.at[k], recv_sem=go_recv.at[k],
                device_id=(sp, to), device_id_type=MESH,
            ).start()

    def first_of(k):
        return (PAIR * k + 2) % layers

    def inner(k, _):
        send_chunk(k, first_of(k))
        return 0

    lax.fori_loop(0, 2, boundary_layer, 0)
    lax.fori_loop(layers - 2, layers, boundary_layer, 0)

    @pl.when((sp > 0) & (sp != cross))
    def _():
        to_left.start()

    @pl.when((sp < spaces - 1) & (sp != cross - 1))
    def _():
        to_right.start()

    @pl.when(sp == cross - 1)
    def _():
        for p in range(cross):
            pltpu.make_async_remote_copy(
                src_ref=piece(layers, p), dst_ref=piece(0, p) if p == 0 else relay,
                send_sem=halo_send.at[1], recv_sem=halo_recv.at[1] if p == 0 else relay_sem.at[0],
                device_id=(cross + p, me), device_id_type=MESH).start()

    @pl.when(sp == cross)
    def _():
        for p in range(cross):
            pltpu.make_async_remote_copy(
                src_ref=piece(2, p), dst_ref=piece(layers + 2, p) if p == cross - 1 else relay,
                send_sem=halo_send.at[0], recv_sem=halo_recv.at[0] if p == cross - 1 else relay_sem.at[0],
                device_id=(p, me), device_id_type=MESH).start()

    lh, ll = high.at[0:2 * FULL], low.at[0:2 * FULL]
    (rh, bh, oh), (rl, bl, ol) = (
        [ref.at[2 * FULL + 256 * i:2 * FULL + 256 * (i + 1)] for i in range(3)] for ref in (high, low))

    def collide(k, _):
        x0 = first_of(k)
        arrived = cells.at[pl.ds(x0, PAIR), pl.ds(0, 240), :]
        pltpu.make_async_copy(arrived, arrived, go_recv.at[k]).wait()
        field = jnp.concatenate([cells[x0], cells[x0 + 1]], 1)
        spec = mul3((lh[...], ll[...]), split(field))
        tc, ts = small[0:FULL, :], small[FULL:2 * FULL, :]
        parts = []
        for i in range(PAIR):
            re = spec[:FULL, 128 * i:128 * i + 128]
            im = spec[FULL:, 128 * i:128 * i + 128]
            parts.append(jnp.concatenate([re * tc + im * ts, im * tc - re * ts], 1))
        spec = mul3(split(jnp.concatenate(parts, 0)), (rh[...], rl[...]))
        tc, ts = small[0:HALF, :], small[FULL:FULL + HALF, :]
        for i in range(PAIR):
            re = spec[FULL * i:FULL * i + HALF, :128].reshape(8, 16, 128)
            im = spec[FULL * i:FULL * i + HALF, 128:].reshape(8, 16, 128)
            re16 = spec[FULL * i + HALF:FULL * (i + 1), :128]
            im16 = spec[FULL * i + HALF:FULL * (i + 1), 128:]
            for t in range(4):
                w = weights[t].reshape(8, 16, 128)
                for r in range(8):
                    w16 = weights16[t, 8 * r:8 * r + 8, :]
                    zr, zi = w[r] * re[r], w[r] * im[r]
                    zr = jnp.concatenate([zr[:8] - w16 * im16[r:r + 1, :], zr[8:]], 0)
                    zi = jnp.concatenate([zi[:8] + w16 * re16[r:r + 1, :], zi[8:]], 0)
                    if t % 2:
                        zr, zi = zi, -zr
                    rows = slice(HALF * (PAIR * t + i) + 16 * r, HALF * (PAIR * t + i) + 16 * r + 16)
                    yh[rows, :], yl[rows, :] = split(jnp.concatenate([zr, zi], 1))
        fields = []
        for t in range(4):
            rows = slice(PAIR * HALF * t, PAIR * HALF * (t + 1))
            value = mul3((yh[rows, :], yl[rows, :]), (bh[...], bl[...]))
            reals, imags = [], []
            for i in range(PAIR):
                re = value[HALF * i:HALF * (i + 1), :128]
                im = value[HALF * i:HALF * (i + 1), 128:]
                reals.append(re * tc - im * ts)
                imags.append(re * ts + im * tc)
            value = jnp.concatenate([jnp.concatenate(reals, 1), jnp.concatenate(imags, 1)], 0)
            fields.append(mul3((oh[...], ol[...]), split(value)))
        value = fields[0] * fields[2] - fields[1] * fields[3]
        for i in range(PAIR):
            done[x0 + i] = cells[x0 + i] + value[:, 128 * i:128 * i + 128]
        for off in ORDER:
            to = partner(me, off)
            pltpu.make_async_remote_copy(
                src_ref=done.at[pl.ds(x0, PAIR), pl.ds(pl.multiple_of(16 * to, 16), 16), :],
                dst_ref=result.at[pl.ds(x0, PAIR), my_y, my_z],
                send_sem=back_send.at[k], recv_sem=back_recv.at[k],
                device_id=(sp, to), device_id_type=MESH,
            ).start()
        return 0

    lax.fori_loop(2, 6, boundary_layer, 0)
    send_chunk(0, first_of(0))

    def bounded(k, _):
        lax.fori_loop(2 * k + 4, 2 * k + 6, boundary_layer, 0)
        return inner(k, 0)

    lax.fori_loop(1, chunks - 3, bounded, 0)

    @pl.when(sp > cross)
    def _():
        pltpu.make_async_copy(relay, relay, relay_sem.at[0]).wait()
        relay_right.start()

    @pl.when(sp < cross - 1)
    def _():
        pltpu.make_async_copy(relay, relay, relay_sem.at[0]).wait()
        relay_left.start()

    inner(chunks - 3, 0)
    prepare()
    lax.fori_loop(0, 1, collide, 0)

    @pl.when(sp > 0)
    def _():
        to_right.wait_recv()

    @pl.when(sp < spaces - 1)
    def _():
        to_left.wait_recv()

    lax.fori_loop(chunks - 2, chunks, inner, 0)

    lax.fori_loop(1, chunks, collide, 0)

    mine = pltpu.make_async_copy(
        done.at[:, own, :], result.at[:, my_y, my_z], own_sem)
    mine.start()

    def finish(k, _):
        x0 = first_of(k)
        block = cells.at[pl.ds(x0, PAIR), pl.ds(0, 240), :]
        pltpu.make_async_copy(block, block, go_send.at[k]).wait()
        pltpu.make_async_copy(block, block, back_send.at[k]).wait()
        pltpu.make_async_copy(block, block, back_recv.at[k]).wait()
        return 0

    lax.fori_loop(0, chunks, finish, 0)
    mine.wait()

    @pl.when(sp > 0)
    def _():
        to_left.wait_send()

    @pl.when(sp < spaces - 1)
    def _():
        to_right.wait_send()

    @pl.when(sp > cross)
    def _():
        relay_right.wait_send()

    @pl.when(sp < cross - 1)
    def _():
        relay_left.wait_send()

    for copy in sends:
        copy.wait_send()


def place_kernel(layers, source, target, held, rows, in_sem, out_sem):
    step = layers // 4

    def load(i):
        return pltpu.make_async_copy(source.at[pl.ds(step * i, step)], held.at[pl.ds(step * i, step)], in_sem.at[i])

    def store(i):
        part = pl.ds(256 * step * i, 256 * step)
        return pltpu.make_async_copy(rows.at[part], target.at[part], out_sem.at[i])

    for i in range(4):
        load(i).start()
    for i in range(4):
        load(i).wait()

        def place(x, _):
            for y in range(4):
                for z in range(4):
                    for e in range(2):
                        rows[pl.ds(256 * x + 64 * y + 32 * e + z, 8, stride=4), :] = held[x, y, z, 8 * e:8 * e + 8, :]
            return 0

        lax.fori_loop(step * i, step * (i + 1), place, 0)
        store(i).start()
    for i in range(4):
        store(i).wait()


def shards(spaces, dist, cell_kind, inflow, wall_shape, gain_tables, second_tables):
    layers = dist.shape[0]
    mats, flips, small = tables()
    rows = dist.reshape(layers, 4, 4, 16, 128).transpose(0, 1, 3, 2, 4).reshape(layers * 256, 128)
    anywhere = pl.BlockSpec(memory_space=pl.ANY)
    chunks = layers // PAIR
    dma = pltpu.SemaphoreType.DMA
    result = pl.pallas_call(
        functools.partial(step_kernel, spaces, layers),
        out_shape=jax.ShapeDtypeStruct((layers, 4, 4, 16, 128), F32),
        in_specs=[anywhere, pl.BlockSpec(memory_space=pltpu.SMEM)] + [anywhere] * 7,
        out_specs=anywhere,
        scratch_shapes=[
            pltpu.VMEM((layers * 256, 128), F32),
            pltpu.VMEM((16, 128), F32), pltpu.VMEM((16, 128), F32),
            pltpu.VMEM((256, 128), F32), pltpu.VMEM((256, 128), F32),
            pltpu.VMEM(mats.shape, F32), pltpu.VMEM(mats.shape, BF16), pltpu.VMEM(mats.shape, BF16), pltpu.VMEM(flips.shape, F32), pltpu.VMEM(small.shape, F32),
            pltpu.VMEM((layers + 4, 4, 4, 16, 128), F32),
            pltpu.VMEM((256, 128), F32),
            pltpu.VMEM((1, 256), F32),
            pltpu.VMEM((16, 1, 256), F32),
            pltpu.VMEM((layers * 16, 128), F32),
            pltpu.VMEM((layers, 16, 16, 128), F32),
            pltpu.VMEM((layers, 256, 128), F32),
            pltpu.VMEM((layers, 256, 128), F32),
            pltpu.VMEM((4, 256, 128), F32),
            pltpu.VMEM((4, HALF, 128), F32),
            pltpu.VMEM((4, 64, 128), F32),
            pltpu.VMEM((4 * PAIR * HALF, 256), BF16),
            pltpu.VMEM((4 * PAIR * HALF, 256), BF16),
            pltpu.VMEM((2, 2, 16, 128), F32),
            dma((8,)), dma((2,)),
            dma((15,)), dma((15,)),
            dma((2,)), dma((2,)),
            dma((chunks,)), dma((chunks,)),
            dma((chunks,)), dma((chunks,)),
            dma,
        ],
        compiler_params=pltpu.CompilerParams(
            collective_id=0, has_side_effects=True, vmem_limit_bytes=56 * 2**20),
    )(
        rows, cell_kind.transpose(1, 2, 0), inflow.reshape(16, 128), wall_shape.reshape(16, 128),
        gain_tables.reshape(256, 128), second_tables.reshape(256, 128),
        jnp.asarray(mats), jnp.asarray(flips), jnp.asarray(small),
    )
    placed = pl.pallas_call(
        functools.partial(place_kernel, layers),
        out_shape=jax.ShapeDtypeStruct((layers * 256, 128), F32),
        in_specs=[anywhere],
        out_specs=anywhere,
        scratch_shapes=[
            pltpu.VMEM((layers, 4, 4, 16, 128), F32), pltpu.VMEM((layers * 256, 128), F32), dma((4,)), dma((4,))],
        compiler_params=pltpu.CompilerParams(vmem_limit_bytes=56 * 2**20),
    )(result)
    return placed.reshape(layers, 4, 16, 4, 128).transpose(0, 1, 3, 2, 4).reshape(dist.shape)


def solution(mesh):
    placed = (P("space", None, None, "vel"), P("space", None, None), P("vel"), P("vel"), P(), P())
    return jax.shard_map(
        functools.partial(shards, mesh.shape["space"]),
        mesh=mesh, in_specs=placed, out_specs=P("space", None, None, "vel"), check_vma=False,
    )
```

```python
import functools
import math

import jax
import jax.numpy as jnp
import numpy as np
from jax import lax
from jax.experimental import pallas as pl
from jax.experimental.pallas import tpu as pltpu
from jax.sharding import PartitionSpec as P

VR = 32
NV = VR * VR * VR
CFL = 0.3
COLLISION_AXIS = 0.25
HIGH = lax.Precision.HIGHEST
MESH = pl.DeviceIdType.MESH
F32 = jnp.float32
BF16 = jnp.bfloat16

FULL = 136
HALF = 128
PAIR = 2

ORDER = (
    (1, 2, 0), (1, 2, 1), (1, 1, 0), (1, 3, 0), (1, 1, 1), (1, 3, 1), (1, 0, 0), (0, 2, 0),
    (1, 0, 1), (0, 2, 1), (0, 1, 0), (0, 3, 0), (0, 1, 1), (0, 3, 1), (0, 0, 1),
)


def tables():
    two_pi = 2.0 * math.pi
    row = np.arange(256)
    a, b_hi = row // 8, row % 8
    spec = np.arange(FULL)
    ka = np.where(spec < HALF, spec % 16, 16)
    r = np.where(spec < HALF, spec // 16, spec - HALF)
    theta = two_pi / 32 * ((ka[:, None] * a[None] + 4 * r[:, None] * b_hi[None]) % 32)
    left = np.concatenate([np.cos(theta), -np.sin(theta)], 0)
    lane = np.arange(128)
    b_lo, c = lane // 32, lane % 32
    angle = two_pi / 32 * ((8 * b_lo[:, None] * b_lo[None] + c[:, None] * c[None]) % 32)
    cos, sin = np.cos(angle), np.sin(angle)
    right = np.block([[cos, -sin], [sin, cos]])
    back = np.block([[cos, sin], [-sin, cos]])
    turn = two_pi / 32 * (r[:, None] * b_lo[None])
    twiddle = np.stack([np.cos(turn), np.sin(turn)])
    th = theta[:HALF].T
    phi = two_pi / 8 * ((r[None, :HALF] * b_hi[:, None]) % 8)
    sign = np.where(a % 2 == 0, 1.0, -1.0)[:, None]
    first = (ka[:HALF] == 0)[None]
    real = np.where(first, np.cos(phi) + sign * np.sin(phi), 2 * np.cos(th))
    imag = np.where(first, -np.sin(phi) + sign * np.cos(phi), -2 * np.sin(th))
    out = np.concatenate([real, imag], 1)
    source = ((-a) % 32) * 8
    flip0 = np.zeros((256, 256), np.float32)
    flip0[row, source + (-b_hi) % 8] = 1
    flip1 = np.zeros((256, 256), np.float32)
    flip1[row, source + (-b_hi - 1) % 8] = 1
    flip_lane = np.zeros((128, 128), np.float32)
    flip_lane[((-b_lo) % 4) * 32 + (-c) % 32, lane] = 1
    flips = np.concatenate([flip0, flip1], 0)
    small = np.concatenate([twiddle.reshape(2 * FULL, 128), flip_lane], 0)
    return np.concatenate([left, right, back, out], 0).astype(np.float32), flips, small.astype(np.float32)


def split(value):
    high = value.astype(BF16)
    return high, (value - high.astype(F32)).astype(BF16)


def mul3(left, right):
    dot = functools.partial(jnp.dot, preferred_element_type=F32)
    return dot(left[0], right[0]) + (dot(left[1], right[0]) + dot(left[0], right[1]))


def minmod(p, q):
    return jnp.maximum(jnp.minimum(p, q), jnp.minimum(jnp.maximum(p, q), 0.0))


def coords(vel):
    return vel // 8, (vel // 2) % 4, vel % 2


def partner(vel, off):
    y, x, core = coords(vel)
    return ((y + off[0]) % 2) * 8 + ((x + off[1]) % 4) * 2 + (core + off[2]) % 2


def step_kernel(
    spaces, layers,
    dist, kind, inflow_hbm, wall_hbm, gain_hbm, second_hbm, mats_hbm, flips_hbm, small_hbm,
    result,
    raw, inflow, wall, gain, second, mats, high, low, flips, small,
    ext, lane_sums, mass_row, mass_all, scales, read, cells, done, nat, weights, weights16, yh, yl,
    relay, in_sem, relay_sem, mass_send, mass_recv, halo_send, halo_recv, go_send, go_recv, back_send, back_recv, own_sem,
):
    sp = lax.axis_index("space")
    me = lax.axis_index("vel")
    my_y, my_z = me // 4, me % 4
    chunks = layers // PAIR
    count = layers * 16
    cross = spaces // 2

    loads = []
    for i, (source, target) in enumerate((
        (dist, raw), (wall_hbm, wall), (gain_hbm, gain), (second_hbm, second), (flips_hbm, flips),
        (small_hbm, small), (mats_hbm, mats), (inflow_hbm, inflow),
    )):
        loads.append(pltpu.make_async_copy(source, target, in_sem.at[i]))
        loads[-1].start()

    barrier = pltpu.get_barrier_semaphore()
    for off in ORDER:
        pl.semaphore_signal(barrier, inc=1, device_id=(sp, partner(me, off)), device_id_type=MESH)
    greeted = 0
    for other in range(spaces):
        ends = other in (cross - 1, cross)
        near = (sp == other - 1) | (sp == other + 1) | (sp == cross - 1) | (sp == cross)
        greet = (sp != other) if ends else near & (sp != other)
        greeted = greeted + jnp.where(greet, 1, 0)

        @pl.when(greet)
        def _():
            pl.semaphore_signal(barrier, inc=1, device_id=(other, me), device_id_type=MESH)

    sub = lax.broadcasted_iota(jnp.int32, (8, 128), 0)
    loads[1].wait()
    lane_sums[count:256, :] = jnp.zeros((256 - count, 128), F32)
    lane_sums[count:count + 1, :] = jnp.sum(wall[...], axis=0, keepdims=True)
    loads[0].wait()

    def sum_layer(x, _):
        pieces = []
        for y in range(4):
            block = raw[pl.ds(pl.multiple_of(256 * x + 64 * y, 64), 64), :].reshape(8, 8, 128)
            block = jnp.sum(block, axis=0)
            pieces.append(block + pltpu.roll(block, 4, 0))
        for i in range(2):
            lane_sums[pl.ds(pl.multiple_of(16 * x + 8 * i, 8), 8), :] = jnp.where(
                sub < 4, pieces[2 * i], pieces[2 * i + 1])
        return 0

    lax.fori_loop(0, layers, sum_layer, 0)
    mass_row[...] = jnp.sum(lane_sums[...].T, axis=0, keepdims=True)
    mass_all[me] = mass_row[...]

    pl.semaphore_wait(barrier, len(ORDER) + greeted)

    sends = []
    for i, off in enumerate(ORDER):
        sends.append(pltpu.make_async_remote_copy(
            src_ref=mass_row, dst_ref=mass_all.at[me], send_sem=mass_send.at[i], recv_sem=mass_recv.at[i],
            device_id=(sp, partner(me, off)), device_id_type=MESH,
        ))
        sends[-1].start()

    lane = lax.broadcasted_iota(jnp.int32, (16, 128), 1) // 32
    lane8 = lax.broadcasted_iota(jnp.int32, (8, 128), 1) // 32

    def prepare():
        for load in loads[2:-1]:
            load.wait()
        flip_lane = small[2 * FULL:, :]
        high[...], low[...] = split(mats[...])
        for t, (table, scale) in enumerate(((gain, 1.0 / NV), (second, COLLISION_AXIS / NV))):
            g = table[...]
            rev = jnp.dot(g, flip_lane, precision=HIGH, preferred_element_type=F32)
            mask = lax.broadcasted_iota(jnp.int32, (256, 128), 1) < 32
            rev0 = jnp.dot(flips[0:256, :], rev, precision=HIGH, preferred_element_type=F32)
            rev1 = jnp.dot(flips[256:512, :], rev, precision=HIGH, preferred_element_type=F32)
            rev = jnp.where(mask, rev0, rev1)
            nat[2 * t] = (0.5 * scale) * (g + rev)
            nat[2 * t + 1] = (0.5 * scale) * (g - rev)

        def order_weights(t, _):
            for r in range(8):
                upper, lower = r // 4, r % 4
                value = jnp.zeros((16, 128), F32)
                value16 = jnp.zeros((8, 128), F32)
                for q in range(4):
                    rows = nat[t, pl.ds(2 * q + upper, 16, stride=8), :]
                    row16 = jnp.broadcast_to(nat[t, pl.ds(128 + 2 * q + upper, 1), :], (8, 128))
                    shift = (32 * (q - lower)) % 128
                    if shift:
                        rows = pltpu.roll(rows, shift, 1)
                        row16 = pltpu.roll(row16, shift, 1)
                    value = jnp.where(lane == q, rows, value)
                    value16 = jnp.where(lane8 == q, row16, value16)
                weights[t, 16 * r:16 * r + 16, :] = value
                weights16[t, 8 * r:8 * r + 8, :] = jnp.where(sub == 0, value16, 0.0)
            return 0

        lax.fori_loop(0, 4, order_weights, 0)

    prepare()
    loads[-1].wait()
    for copy in sends:
        copy.wait_recv()
    total = jnp.sum(mass_all[...], axis=0)
    totals = jnp.broadcast_to(total, (128, 256)).T
    scales[...] = totals[:count] / totals[count:count + 1]

    def boundary_layer(x, _):
        for y in range(4):
            for z in range(4):
                what = jnp.full((8, 128), kind[y, z, x], jnp.int32)
                scale = jnp.broadcast_to(scales[pl.ds(x * 16 + 4 * y + z, 1), :], (8, 128))
                for e in range(2):
                    rows = slice(8 * e, 8 * e + 8)
                    value = raw[pl.ds(256 * x + 64 * y + 32 * e + z, 8, stride=4), :]
                    value = jnp.where(what == 1, scale * wall[rows, :], value)
                    ext[2 + x, y, z, rows, :] = jnp.where(what == 2, inflow[rows, :], value)
        return 0

    to_left = pltpu.make_async_remote_copy(
        src_ref=ext.at[pl.ds(2, 2)], dst_ref=ext.at[pl.ds(layers + 2, 2)],
        send_sem=halo_send.at[0], recv_sem=halo_recv.at[0],
        device_id=(lax.rem(sp + spaces - 1, spaces), me), device_id_type=MESH)
    to_right = pltpu.make_async_remote_copy(
        src_ref=ext.at[pl.ds(layers, 2)], dst_ref=ext.at[pl.ds(0, 2)],
        send_sem=halo_send.at[1], recv_sem=halo_recv.at[1],
        device_id=(lax.rem(sp + 1, spaces), me), device_id_type=MESH)

    def piece(x, p):
        return ext.at[pl.ds(x, 2), p // 2, pl.ds(2 * (p % 2), 2)]

    up = lax.rem(sp, cross)
    relay_right = pltpu.make_async_remote_copy(
        src_ref=relay, dst_ref=piece(0, up), send_sem=relay_sem.at[1], recv_sem=halo_recv.at[1],
        device_id=(cross, me), device_id_type=MESH)
    relay_left = pltpu.make_async_remote_copy(
        src_ref=relay, dst_ref=piece(layers + 2, up), send_sem=relay_sem.at[1], recv_sem=halo_recv.at[0],
        device_id=(cross - 1, me), device_id_type=MESH)

    @pl.when(sp == 0)
    def _():
        ext[0:2] = jnp.zeros((2, 4, 4, 16, 128), F32)

    @pl.when(sp == spaces - 1)
    def _():
        ext[layers + 2:layers + 4] = jnp.zeros((2, 4, 4, 16, 128), F32)


    b_index = 4 * lax.broadcasted_iota(jnp.int32, (8, 128), 0) + lane8
    c_index = lax.broadcasted_iota(jnp.int32, (8, 128), 1) % 32

    def speed(index):
        return CFL * (2 * index - (VR - 1)).astype(F32) / (VR - 1)

    nu_y, nu_z = speed(b_index), speed(c_index)
    up_y, up_z = nu_y > 0, nu_z > 0
    size_y, size_z = jnp.abs(nu_y), jnp.abs(nu_z)
    coef_y = jnp.where(up_y, 0.5, -0.5) * (1.0 - size_y)
    coef_z = jnp.where(up_z, 0.5, -0.5) * (1.0 - size_z)

    def ring(s, coef, up, size):
        diff = [s[(i + 1) % 4] - s[i] for i in range(4)]
        face = [s[i] + coef * minmod(diff[i - 1], diff[i]) for i in range(4)]
        step = [face[(i + 1) % 4] - face[i] for i in range(4)]
        return [size * jnp.where(up, step[i - 1], -step[i]) for i in range(4)]

    def transport(x0):
        for e in range(2):
            rows = slice(8 * e, 8 * e + 8)
            nu_x = speed(jnp.full((8, 128), 2 * me + e, jnp.int32))
            up_x = nu_x > 0
            size_x = jnp.abs(nu_x)
            coef_x = jnp.where(up_x, 0.5, -0.5) * (1.0 - size_x)
            for y in range(4):
                for z in range(4):
                    s = [ext[x0 + i, y, z, rows, :] for i in range(6)]
                    diff = [s[i + 1] - s[i] for i in range(5)]
                    face = [s[i + 1] + coef_x * minmod(diff[i], diff[i + 1]) for i in range(4)]
                    step = [face[i + 1] - face[i] for i in range(3)]
                    for i in range(PAIR):
                        read[x0 + i, 4 * y + z, rows, :] = s[i + 2] - size_x * jnp.where(up_x, step[i], -step[i + 1])
            for i in range(PAIR):
                s = [[ext[x0 + 2 + i, y, z, rows, :] for z in range(4)] for y in range(4)]
                along_z = [ring(s[y], coef_z, up_z, size_z) for y in range(4)]
                along_y = [ring([s[y][z] for y in range(4)], coef_y, up_y, size_y) for z in range(4)]
                for y in range(4):
                    for z in range(4):
                        read[x0 + i, 4 * y + z, rows, :] -= along_z[y][z] + along_y[z][y]

    own = pl.ds(pl.multiple_of(16 * me, 16), 16)

    def send_chunk(k, x0):
        transport(x0)
        for i in range(PAIR):
            cells[x0 + i, own, :] = read[x0 + i, me]
        for off in ORDER:
            to = partner(me, off)
            pltpu.make_async_remote_copy(
                src_ref=read.at[pl.ds(x0, PAIR), to], dst_ref=cells.at[pl.ds(x0, PAIR), own, :],
                send_sem=go_send.at[k], recv_sem=go_recv.at[k],
                device_id=(sp, to), device_id_type=MESH,
            ).start()

    def first_of(k):
        return (PAIR * k + 2) % layers

    def inner(k, _):
        send_chunk(k, first_of(k))
        return 0

    lax.fori_loop(0, 2, boundary_layer, 0)
    lax.fori_loop(layers - 2, layers, boundary_layer, 0)

    @pl.when((sp > 0) & (sp != cross))
    def _():
        to_left.start()

    @pl.when((sp < spaces - 1) & (sp != cross - 1))
    def _():
        to_right.start()

    @pl.when(sp == cross - 1)
    def _():
        for p in range(cross):
            pltpu.make_async_remote_copy(
                src_ref=piece(layers, p), dst_ref=piece(0, p) if p == 0 else relay,
                send_sem=halo_send.at[1], recv_sem=halo_recv.at[1] if p == 0 else relay_sem.at[0],
                device_id=(cross + p, me), device_id_type=MESH).start()

    @pl.when(sp == cross)
    def _():
        for p in range(cross):
            pltpu.make_async_remote_copy(
                src_ref=piece(2, p), dst_ref=piece(layers + 2, p) if p == cross - 1 else relay,
                send_sem=halo_send.at[0], recv_sem=halo_recv.at[0] if p == cross - 1 else relay_sem.at[0],
                device_id=(p, me), device_id_type=MESH).start()

    lh, ll = high.at[0:2 * FULL], low.at[0:2 * FULL]
    (rh, bh, oh), (rl, bl, ol) = (
        [ref.at[2 * FULL + 256 * i:2 * FULL + 256 * (i + 1)] for i in range(3)] for ref in (high, low))

    def collide(k, _):
        x0 = first_of(k)
        arrived = cells.at[pl.ds(x0, PAIR), pl.ds(0, 240), :]
        pltpu.make_async_copy(arrived, arrived, go_recv.at[k]).wait()
        field = jnp.concatenate([cells[x0], cells[x0 + 1]], 1)
        spec = mul3((lh[...], ll[...]), split(field))
        tc, ts = small[0:FULL, :], small[FULL:2 * FULL, :]
        parts = []
        for i in range(PAIR):
            re = spec[:FULL, 128 * i:128 * i + 128]
            im = spec[FULL:, 128 * i:128 * i + 128]
            parts.append(jnp.concatenate([re * tc + im * ts, im * tc - re * ts], 1))
        spec = mul3(split(jnp.concatenate(parts, 0)), (rh[...], rl[...]))
        tc, ts = small[0:HALF, :], small[FULL:FULL + HALF, :]
        for i in range(PAIR):
            re = spec[FULL * i:FULL * i + HALF, :128].reshape(8, 16, 128)
            im = spec[FULL * i:FULL * i + HALF, 128:].reshape(8, 16, 128)
            re16 = spec[FULL * i + HALF:FULL * (i + 1), :128]
            im16 = spec[FULL * i + HALF:FULL * (i + 1), 128:]
            for t in range(4):
                w = weights[t].reshape(8, 16, 128)
                for r in range(8):
                    w16 = weights16[t, 8 * r:8 * r + 8, :]
                    zr, zi = w[r] * re[r], w[r] * im[r]
                    zr = jnp.concatenate([zr[:8] - w16 * im16[r:r + 1, :], zr[8:]], 0)
                    zi = jnp.concatenate([zi[:8] + w16 * re16[r:r + 1, :], zi[8:]], 0)
                    if t % 2:
                        zr, zi = zi, -zr
                    rows = slice(HALF * (PAIR * t + i) + 16 * r, HALF * (PAIR * t + i) + 16 * r + 16)
                    yh[rows, :], yl[rows, :] = split(jnp.concatenate([zr, zi], 1))
        fields = []
        for t in range(4):
            rows = slice(PAIR * HALF * t, PAIR * HALF * (t + 1))
            value = mul3((yh[rows, :], yl[rows, :]), (bh[...], bl[...]))
            reals, imags = [], []
            for i in range(PAIR):
                re = value[HALF * i:HALF * (i + 1), :128]
                im = value[HALF * i:HALF * (i + 1), 128:]
                reals.append(re * tc - im * ts)
                imags.append(re * ts + im * tc)
            value = jnp.concatenate([jnp.concatenate(reals, 1), jnp.concatenate(imags, 1)], 0)
            fields.append(mul3((oh[...], ol[...]), split(value)))
        value = fields[0] * fields[2] - fields[1] * fields[3]
        for i in range(PAIR):
            done[x0 + i] = cells[x0 + i] + value[:, 128 * i:128 * i + 128]
        for off in ORDER:
            to = partner(me, off)
            pltpu.make_async_remote_copy(
                src_ref=done.at[pl.ds(x0, PAIR), pl.ds(pl.multiple_of(16 * to, 16), 16), :],
                dst_ref=result.at[pl.ds(x0, PAIR), my_y, my_z],
                send_sem=back_send.at[k], recv_sem=back_recv.at[k],
                device_id=(sp, to), device_id_type=MESH,
            ).start()
        return 0

    lax.fori_loop(2, 6, boundary_layer, 0)
    send_chunk(0, first_of(0))

    def bounded(k, _):
        lax.fori_loop(2 * k + 4, 2 * k + 6, boundary_layer, 0)
        return inner(k, 0)

    lax.fori_loop(1, chunks - 3, bounded, 0)

    @pl.when(sp > cross)
    def _():
        pltpu.make_async_copy(relay, relay, relay_sem.at[0]).wait()
        relay_right.start()

    @pl.when(sp < cross - 1)
    def _():
        pltpu.make_async_copy(relay, relay, relay_sem.at[0]).wait()
        relay_left.start()

    inner(chunks - 3, 0)
    lax.fori_loop(0, 1, collide, 0)

    @pl.when(sp > 0)
    def _():
        to_right.wait_recv()

    @pl.when(sp < spaces - 1)
    def _():
        to_left.wait_recv()

    lax.fori_loop(chunks - 2, chunks, inner, 0)

    lax.fori_loop(1, chunks, collide, 0)

    mine = pltpu.make_async_copy(
        done.at[:, own, :], result.at[:, my_y, my_z], own_sem)
    mine.start()

    def finish(k, _):
        x0 = first_of(k)
        block = cells.at[pl.ds(x0, PAIR), pl.ds(0, 240), :]
        pltpu.make_async_copy(block, block, go_send.at[k]).wait()
        pltpu.make_async_copy(block, block, back_send.at[k]).wait()
        pltpu.make_async_copy(block, block, back_recv.at[k]).wait()
        return 0

    lax.fori_loop(0, chunks, finish, 0)
    mine.wait()

    @pl.when(sp > 0)
    def _():
        to_left.wait_send()

    @pl.when(sp < spaces - 1)
    def _():
        to_right.wait_send()

    @pl.when(sp > cross)
    def _():
        relay_right.wait_send()

    @pl.when(sp < cross - 1)
    def _():
        relay_left.wait_send()

    for copy in sends:
        copy.wait_send()


def place_kernel(layers, source, target, held, rows, in_sem, out_sem):
    step = layers // 4

    def load(i):
        return pltpu.make_async_copy(source.at[pl.ds(step * i, step)], held.at[pl.ds(step * i, step)], in_sem.at[i])

    def store(i):
        part = pl.ds(256 * step * i, 256 * step)
        return pltpu.make_async_copy(rows.at[part], target.at[part], out_sem.at[i])

    for i in range(4):
        load(i).start()
    for i in range(4):
        load(i).wait()

        def place(x, _):
            for y in range(4):
                for z in range(4):
                    for e in range(2):
                        rows[pl.ds(256 * x + 64 * y + 32 * e + z, 8, stride=4), :] = held[x, y, z, 8 * e:8 * e + 8, :]
            return 0

        lax.fori_loop(step * i, step * (i + 1), place, 0)
        store(i).start()
    for i in range(4):
        store(i).wait()


def shards(spaces, dist, cell_kind, inflow, wall_shape, gain_tables, second_tables):
    layers = dist.shape[0]
    mats, flips, small = tables()
    rows = dist.reshape(layers, 4, 4, 16, 128).transpose(0, 1, 3, 2, 4).reshape(layers * 256, 128)
    anywhere = pl.BlockSpec(memory_space=pl.ANY)
    chunks = layers // PAIR
    dma = pltpu.SemaphoreType.DMA
    result = pl.pallas_call(
        functools.partial(step_kernel, spaces, layers),
        out_shape=jax.ShapeDtypeStruct((layers, 4, 4, 16, 128), F32),
        in_specs=[anywhere, pl.BlockSpec(memory_space=pltpu.SMEM)] + [anywhere] * 7,
        out_specs=anywhere,
        scratch_shapes=[
            pltpu.VMEM((layers * 256, 128), F32),
            pltpu.VMEM((16, 128), F32), pltpu.VMEM((16, 128), F32),
            pltpu.VMEM((256, 128), F32), pltpu.VMEM((256, 128), F32),
            pltpu.VMEM(mats.shape, F32), pltpu.VMEM(mats.shape, BF16), pltpu.VMEM(mats.shape, BF16), pltpu.VMEM(flips.shape, F32), pltpu.VMEM(small.shape, F32),
            pltpu.VMEM((layers + 4, 4, 4, 16, 128), F32),
            pltpu.VMEM((256, 128), F32),
            pltpu.VMEM((1, 256), F32),
            pltpu.VMEM((16, 1, 256), F32),
            pltpu.VMEM((layers * 16, 128), F32),
            pltpu.VMEM((layers, 16, 16, 128), F32),
            pltpu.VMEM((layers, 256, 128), F32),
            pltpu.VMEM((layers, 256, 128), F32),
            pltpu.VMEM((4, 256, 128), F32),
            pltpu.VMEM((4, HALF, 128), F32),
            pltpu.VMEM((4, 64, 128), F32),
            pltpu.VMEM((4 * PAIR * HALF, 256), BF16),
            pltpu.VMEM((4 * PAIR * HALF, 256), BF16),
            pltpu.VMEM((2, 2, 16, 128), F32),
            dma((8,)), dma((2,)),
            dma((15,)), dma((15,)),
            dma((2,)), dma((2,)),
            dma((chunks,)), dma((chunks,)),
            dma((chunks,)), dma((chunks,)),
            dma,
        ],
        compiler_params=pltpu.CompilerParams(
            collective_id=0, has_side_effects=True, vmem_limit_bytes=56 * 2**20),
    )(
        rows, cell_kind.transpose(1, 2, 0), inflow.reshape(16, 128), wall_shape.reshape(16, 128),
        gain_tables.reshape(256, 128), second_tables.reshape(256, 128),
        jnp.asarray(mats), jnp.asarray(flips), jnp.asarray(small),
    )
    placed = pl.pallas_call(
        functools.partial(place_kernel, layers),
        out_shape=jax.ShapeDtypeStruct((layers * 256, 128), F32),
        in_specs=[anywhere],
        out_specs=anywhere,
        scratch_shapes=[
            pltpu.VMEM((layers, 4, 4, 16, 128), F32), pltpu.VMEM((layers * 256, 128), F32), dma((4,)), dma((4,))],
        compiler_params=pltpu.CompilerParams(vmem_limit_bytes=56 * 2**20),
    )(result)
    return placed.reshape(layers, 4, 16, 4, 128).transpose(0, 1, 3, 2, 4).reshape(dist.shape)


def solution(mesh):
    placed = (P("space", None, None, "vel"), P("space", None, None), P("vel"), P("vel"), P(), P())
    return jax.shard_map(
        functools.partial(shards, mesh.shape["space"]),
        mesh=mesh, in_specs=placed, out_specs=P("space", None, None, "vel"), check_vma=False,
    )
```

```python
import functools
import math

import jax
import jax.numpy as jnp
import numpy as np
from jax import lax
from jax.experimental import pallas as pl
from jax.experimental.pallas import tpu as pltpu
from jax.sharding import PartitionSpec as P

VR = 32
NV = VR * VR * VR
CFL = 0.3
COLLISION_AXIS = 0.25
HIGH = lax.Precision.HIGHEST
MESH = pl.DeviceIdType.MESH
F32 = jnp.float32
BF16 = jnp.bfloat16

FULL = 136
HALF = 128
PAIR = 2

ORDER = (
    (1, 2, 0), (1, 2, 1), (1, 1, 0), (1, 3, 0), (1, 1, 1), (1, 3, 1), (1, 0, 0), (0, 2, 0),
    (1, 0, 1), (0, 2, 1), (0, 1, 0), (0, 3, 0), (0, 1, 1), (0, 3, 1), (0, 0, 1),
)


def tables():
    two_pi = 2.0 * math.pi
    row = np.arange(256)
    a, b_hi = row // 8, row % 8
    spec = np.arange(FULL)
    ka = np.where(spec < HALF, spec % 16, 16)
    r = np.where(spec < HALF, spec // 16, spec - HALF)
    theta = two_pi / 32 * ((ka[:, None] * a[None] + 4 * r[:, None] * b_hi[None]) % 32)
    left = np.concatenate([np.cos(theta), -np.sin(theta)], 0)
    lane = np.arange(128)
    b_lo, c = lane // 32, lane % 32
    angle = two_pi / 32 * ((8 * b_lo[:, None] * b_lo[None] + c[:, None] * c[None]) % 32)
    cos, sin = np.cos(angle), np.sin(angle)
    right = np.block([[cos, -sin], [sin, cos]])
    back = np.block([[cos, sin], [-sin, cos]])
    turn = two_pi / 32 * (r[:, None] * b_lo[None])
    twiddle = np.stack([np.cos(turn), np.sin(turn)])
    th = theta[:HALF].T
    phi = two_pi / 8 * ((r[None, :HALF] * b_hi[:, None]) % 8)
    sign = np.where(a % 2 == 0, 1.0, -1.0)[:, None]
    first = (ka[:HALF] == 0)[None]
    real = np.where(first, np.cos(phi) + sign * np.sin(phi), 2 * np.cos(th))
    imag = np.where(first, -np.sin(phi) + sign * np.cos(phi), -2 * np.sin(th))
    out = np.concatenate([real, imag], 1)
    source = ((-a) % 32) * 8
    flip0 = np.zeros((256, 256), np.float32)
    flip0[row, source + (-b_hi) % 8] = 1
    flip1 = np.zeros((256, 256), np.float32)
    flip1[row, source + (-b_hi - 1) % 8] = 1
    flip_lane = np.zeros((128, 128), np.float32)
    flip_lane[((-b_lo) % 4) * 32 + (-c) % 32, lane] = 1
    flips = np.concatenate([flip0, flip1], 0)
    small = np.concatenate([twiddle.reshape(2 * FULL, 128), flip_lane], 0)
    return np.concatenate([left, right, back, out], 0).astype(np.float32), flips, small.astype(np.float32)


def split(value):
    high = value.astype(BF16)
    return high, (value - high.astype(F32)).astype(BF16)


def mul3(left, right):
    dot = functools.partial(jnp.dot, preferred_element_type=F32)
    return dot(left[0], right[0]) + (dot(left[1], right[0]) + dot(left[0], right[1]))


def minmod(p, q):
    return jnp.maximum(jnp.minimum(p, q), jnp.minimum(jnp.maximum(p, q), 0.0))


def coords(vel):
    return vel // 8, (vel // 2) % 4, vel % 2


def partner(vel, off):
    y, x, core = coords(vel)
    return ((y + off[0]) % 2) * 8 + ((x + off[1]) % 4) * 2 + (core + off[2]) % 2


def step_kernel(
    spaces, layers,
    dist, kind, inflow_hbm, wall_hbm, gain_hbm, second_hbm, mats_hbm, flips_hbm, small_hbm,
    result,
    raw, inflow, wall, gain, second, mats, high, low, flips, small,
    ext, lane_sums, mass_row, mass_all, scales, read, cells, done, nat, weights, weights16, yh, yl,
    relay, in_sem, relay_sem, mass_send, mass_recv, halo_send, halo_recv, go_send, go_recv, back_send, back_recv, own_sem,
):
    sp = lax.axis_index("space")
    me = lax.axis_index("vel")
    my_y, my_z = me // 4, me % 4
    chunks = layers // PAIR
    count = layers * 16
    cross = spaces // 2

    loads = []
    for i, (source, target) in enumerate((
        (dist, raw), (wall_hbm, wall), (gain_hbm, gain), (second_hbm, second), (flips_hbm, flips),
        (small_hbm, small), (mats_hbm, mats), (inflow_hbm, inflow),
    )):
        loads.append(pltpu.make_async_copy(source, target, in_sem.at[i]))
        loads[-1].start()

    barrier = pltpu.get_barrier_semaphore()
    for off in ORDER:
        pl.semaphore_signal(barrier, inc=1, device_id=(sp, partner(me, off)), device_id_type=MESH)
    greeted = 0
    for other in range(spaces):
        ends = other in (cross - 1, cross)
        near = (sp == other - 1) | (sp == other + 1) | (sp == cross - 1) | (sp == cross)
        greet = (sp != other) if ends else near & (sp != other)
        greeted = greeted + jnp.where(greet, 1, 0)

        @pl.when(greet)
        def _():
            pl.semaphore_signal(barrier, inc=1, device_id=(other, me), device_id_type=MESH)

    sub = lax.broadcasted_iota(jnp.int32, (8, 128), 0)
    loads[1].wait()
    lane_sums[count:256, :] = jnp.zeros((256 - count, 128), F32)
    lane_sums[count:count + 1, :] = jnp.sum(wall[...], axis=0, keepdims=True)
    loads[0].wait()

    def sum_layer(x, _):
        pieces = []
        for y in range(4):
            block = raw[pl.ds(pl.multiple_of(256 * x + 64 * y, 64), 64), :].reshape(8, 8, 128)
            block = jnp.sum(block, axis=0)
            pieces.append(block + pltpu.roll(block, 4, 0))
        for i in range(2):
            lane_sums[pl.ds(pl.multiple_of(16 * x + 8 * i, 8), 8), :] = jnp.where(
                sub < 4, pieces[2 * i], pieces[2 * i + 1])
        return 0

    lax.fori_loop(0, layers, sum_layer, 0)
    mass_row[...] = jnp.sum(lane_sums[...].T, axis=0, keepdims=True)
    mass_all[me] = mass_row[...]

    pl.semaphore_wait(barrier, len(ORDER) + greeted)

    sends = []
    for i, off in enumerate(ORDER):
        sends.append(pltpu.make_async_remote_copy(
            src_ref=mass_row, dst_ref=mass_all.at[me], send_sem=mass_send.at[i], recv_sem=mass_recv.at[i],
            device_id=(sp, partner(me, off)), device_id_type=MESH,
        ))
        sends[-1].start()

    lane = lax.broadcasted_iota(jnp.int32, (16, 128), 1) // 32
    lane8 = lax.broadcasted_iota(jnp.int32, (8, 128), 1) // 32

    def prepare():
        for load in loads[2:-1]:
            load.wait()
        flip_lane = small[2 * FULL:, :]
        high[...], low[...] = split(mats[...])
        for t, (table, scale) in enumerate(((gain, 1.0 / NV), (second, COLLISION_AXIS / NV))):
            g = table[...]
            rev = jnp.dot(g, flip_lane, precision=HIGH, preferred_element_type=F32)
            mask = lax.broadcasted_iota(jnp.int32, (256, 128), 1) < 32
            rev0 = jnp.dot(flips[0:256, :], rev, precision=HIGH, preferred_element_type=F32)
            rev1 = jnp.dot(flips[256:512, :], rev, precision=HIGH, preferred_element_type=F32)
            rev = jnp.where(mask, rev0, rev1)
            nat[2 * t] = (0.5 * scale) * (g + rev)
            nat[2 * t + 1] = (0.5 * scale) * (g - rev)

        def order_weights(t, _):
            for r in range(8):
                upper, lower = r // 4, r % 4
                value = jnp.zeros((16, 128), F32)
                value16 = jnp.zeros((8, 128), F32)
                for q in range(4):
                    rows = nat[t, pl.ds(2 * q + upper, 16, stride=8), :]
                    row16 = jnp.broadcast_to(nat[t, pl.ds(128 + 2 * q + upper, 1), :], (8, 128))
                    shift = (32 * (q - lower)) % 128
                    if shift:
                        rows = pltpu.roll(rows, shift, 1)
                        row16 = pltpu.roll(row16, shift, 1)
                    value = jnp.where(lane == q, rows, value)
                    value16 = jnp.where(lane8 == q, row16, value16)
                weights[t, 16 * r:16 * r + 16, :] = value
                weights16[t, 8 * r:8 * r + 8, :] = jnp.where(sub == 0, value16, 0.0)
            return 0

        lax.fori_loop(0, 4, order_weights, 0)

    prepare()
    loads[-1].wait()
    for copy in sends:
        copy.wait_recv()
    total = jnp.sum(mass_all[...], axis=0)
    totals = jnp.broadcast_to(total, (128, 256)).T
    scales[...] = totals[:count] / totals[count:count + 1]

    def boundary_layer(x, _):
        for y in range(4):
            for z in range(4):
                what = jnp.full((8, 128), kind[y, z, x], jnp.int32)
                scale = jnp.broadcast_to(scales[pl.ds(x * 16 + 4 * y + z, 1), :], (8, 128))
                for e in range(2):
                    rows = slice(8 * e, 8 * e + 8)
                    value = raw[pl.ds(256 * x + 64 * y + 32 * e + z, 8, stride=4), :]
                    value = jnp.where(what == 1, scale * wall[rows, :], value)
                    ext[2 + x, y, z, rows, :] = jnp.where(what == 2, inflow[rows, :], value)
        return 0

    to_left = pltpu.make_async_remote_copy(
        src_ref=ext.at[pl.ds(2, 2)], dst_ref=ext.at[pl.ds(layers + 2, 2)],
        send_sem=halo_send.at[0], recv_sem=halo_recv.at[0],
        device_id=(lax.rem(sp + spaces - 1, spaces), me), device_id_type=MESH)
    to_right = pltpu.make_async_remote_copy(
        src_ref=ext.at[pl.ds(layers, 2)], dst_ref=ext.at[pl.ds(0, 2)],
        send_sem=halo_send.at[1], recv_sem=halo_recv.at[1],
        device_id=(lax.rem(sp + 1, spaces), me), device_id_type=MESH)

    def piece(x, p):
        return ext.at[pl.ds(x, 2), p // 2, pl.ds(2 * (p % 2), 2)]

    up = lax.rem(sp, cross)
    relay_right = pltpu.make_async_remote_copy(
        src_ref=relay, dst_ref=piece(0, up), send_sem=relay_sem.at[1], recv_sem=halo_recv.at[1],
        device_id=(cross, me), device_id_type=MESH)
    relay_left = pltpu.make_async_remote_copy(
        src_ref=relay, dst_ref=piece(layers + 2, up), send_sem=relay_sem.at[1], recv_sem=halo_recv.at[0],
        device_id=(cross - 1, me), device_id_type=MESH)

    @pl.when(sp == 0)
    def _():
        ext[0:2] = jnp.zeros((2, 4, 4, 16, 128), F32)

    @pl.when(sp == spaces - 1)
    def _():
        ext[layers + 2:layers + 4] = jnp.zeros((2, 4, 4, 16, 128), F32)


    b_index = 4 * lax.broadcasted_iota(jnp.int32, (8, 128), 0) + lane8
    c_index = lax.broadcasted_iota(jnp.int32, (8, 128), 1) % 32

    def speed(index):
        return CFL * (2 * index - (VR - 1)).astype(F32) / (VR - 1)

    nu_y, nu_z = speed(b_index), speed(c_index)
    up_y, up_z = nu_y > 0, nu_z > 0
    size_y, size_z = jnp.abs(nu_y), jnp.abs(nu_z)
    coef_y = jnp.where(up_y, 0.5, -0.5) * (1.0 - size_y)
    coef_z = jnp.where(up_z, 0.5, -0.5) * (1.0 - size_z)

    def ring(s, coef, up, size):
        diff = [s[(i + 1) % 4] - s[i] for i in range(4)]
        face = [s[i] + coef * minmod(diff[i - 1], diff[i]) for i in range(4)]
        step = [face[(i + 1) % 4] - face[i] for i in range(4)]
        return [size * jnp.where(up, step[i - 1], -step[i]) for i in range(4)]

    def transport(x0):
        for e in range(2):
            rows = slice(8 * e, 8 * e + 8)
            nu_x = speed(jnp.full((8, 128), 2 * me + e, jnp.int32))
            up_x = nu_x > 0
            size_x = jnp.abs(nu_x)
            coef_x = jnp.where(up_x, 0.5, -0.5) * (1.0 - size_x)
            for y in range(4):
                for z in range(4):
                    s = [ext[x0 + i, y, z, rows, :] for i in range(6)]
                    diff = [s[i + 1] - s[i] for i in range(5)]
                    face = [s[i + 1] + coef_x * minmod(diff[i], diff[i + 1]) for i in range(4)]
                    step = [face[i + 1] - face[i] for i in range(3)]
                    for i in range(PAIR):
                        read[x0 + i, 4 * y + z, rows, :] = s[i + 2] - size_x * jnp.where(up_x, step[i], -step[i + 1])
            for i in range(PAIR):
                s = [[ext[x0 + 2 + i, y, z, rows, :] for z in range(4)] for y in range(4)]
                along_z = [ring(s[y], coef_z, up_z, size_z) for y in range(4)]
                along_y = [ring([s[y][z] for y in range(4)], coef_y, up_y, size_y) for z in range(4)]
                for y in range(4):
                    for z in range(4):
                        read[x0 + i, 4 * y + z, rows, :] -= along_z[y][z] + along_y[z][y]

    own = pl.ds(pl.multiple_of(16 * me, 16), 16)

    def send_chunk(k, x0):
        transport(x0)
        for i in range(PAIR):
            cells[x0 + i, own, :] = read[x0 + i, me]
        for off in ORDER:
            to = partner(me, off)
            pltpu.make_async_remote_copy(
                src_ref=read.at[pl.ds(x0, PAIR), to], dst_ref=cells.at[pl.ds(x0, PAIR), own, :],
                send_sem=go_send.at[k], recv_sem=go_recv.at[k],
                device_id=(sp, to), device_id_type=MESH,
            ).start()

    def first_of(k):
        return (PAIR * k + 2) % layers

    def inner(k, _):
        send_chunk(k, first_of(k))
        return 0

    lax.fori_loop(0, 2, boundary_layer, 0)
    lax.fori_loop(layers - 2, layers, boundary_layer, 0)

    @pl.when((sp > 0) & (sp != cross))
    def _():
        to_left.start()

    @pl.when((sp < spaces - 1) & (sp != cross - 1))
    def _():
        to_right.start()

    @pl.when(sp == cross - 1)
    def _():
        for p in range(cross):
            pltpu.make_async_remote_copy(
                src_ref=piece(layers, p), dst_ref=piece(0, p) if p == 0 else relay,
                send_sem=halo_send.at[1], recv_sem=halo_recv.at[1] if p == 0 else relay_sem.at[0],
                device_id=(cross + p, me), device_id_type=MESH).start()

    @pl.when(sp == cross)
    def _():
        for p in range(cross):
            pltpu.make_async_remote_copy(
                src_ref=piece(2, p), dst_ref=piece(layers + 2, p) if p == cross - 1 else relay,
                send_sem=halo_send.at[0], recv_sem=halo_recv.at[0] if p == cross - 1 else relay_sem.at[0],
                device_id=(p, me), device_id_type=MESH).start()

    lh, ll = high.at[0:2 * FULL], low.at[0:2 * FULL]
    (rh, bh, oh), (rl, bl, ol) = (
        [ref.at[2 * FULL + 256 * i:2 * FULL + 256 * (i + 1)] for i in range(3)] for ref in (high, low))

    def collide(k, _):
        x0 = first_of(k)
        arrived = cells.at[pl.ds(x0, PAIR), pl.ds(0, 240), :]
        pltpu.make_async_copy(arrived, arrived, go_recv.at[k]).wait()
        field = jnp.concatenate([cells[x0], cells[x0 + 1]], 1)
        spec = mul3((lh[...], ll[...]), split(field))
        tc, ts = small[0:FULL, :], small[FULL:2 * FULL, :]
        parts = []
        for i in range(PAIR):
            re = spec[:FULL, 128 * i:128 * i + 128]
            im = spec[FULL:, 128 * i:128 * i + 128]
            parts.append(jnp.concatenate([re * tc + im * ts, im * tc - re * ts], 1))
        spec = mul3(split(jnp.concatenate(parts, 0)), (rh[...], rl[...]))
        tc, ts = small[0:HALF, :], small[FULL:FULL + HALF, :]
        for i in range(PAIR):
            re = spec[FULL * i:FULL * i + HALF, :128].reshape(8, 16, 128)
            im = spec[FULL * i:FULL * i + HALF, 128:].reshape(8, 16, 128)
            re16 = spec[FULL * i + HALF:FULL * (i + 1), :128]
            im16 = spec[FULL * i + HALF:FULL * (i + 1), 128:]
            for t in range(4):
                w = weights[t].reshape(8, 16, 128)
                for r in range(8):
                    w16 = weights16[t, 8 * r:8 * r + 8, :]
                    zr, zi = w[r] * re[r], w[r] * im[r]
                    zr = jnp.concatenate([zr[:8] - w16 * im16[r:r + 1, :], zr[8:]], 0)
                    zi = jnp.concatenate([zi[:8] + w16 * re16[r:r + 1, :], zi[8:]], 0)
                    if t % 2:
                        zr, zi = zi, -zr
                    rows = slice(HALF * (PAIR * t + i) + 16 * r, HALF * (PAIR * t + i) + 16 * r + 16)
                    yh[rows, :], yl[rows, :] = split(jnp.concatenate([zr, zi], 1))
        fields = []
        for t in range(4):
            rows = slice(PAIR * HALF * t, PAIR * HALF * (t + 1))
            value = mul3((yh[rows, :], yl[rows, :]), (bh[...], bl[...]))
            reals, imags = [], []
            for i in range(PAIR):
                re = value[HALF * i:HALF * (i + 1), :128]
                im = value[HALF * i:HALF * (i + 1), 128:]
                reals.append(re * tc - im * ts)
                imags.append(re * ts + im * tc)
            value = jnp.concatenate([jnp.concatenate(reals, 1), jnp.concatenate(imags, 1)], 0)
            fields.append(mul3((oh[...], ol[...]), split(value)))
        value = fields[0] * fields[2] - fields[1] * fields[3]
        for i in range(PAIR):
            done[x0 + i] = cells[x0 + i] + value[:, 128 * i:128 * i + 128]
        for off in ORDER:
            to = partner(me, off)
            pltpu.make_async_remote_copy(
                src_ref=done.at[pl.ds(x0, PAIR), pl.ds(pl.multiple_of(16 * to, 16), 16), :],
                dst_ref=result.at[pl.ds(x0, PAIR), my_y, my_z],
                send_sem=back_send.at[k], recv_sem=back_recv.at[k],
                device_id=(sp, to), device_id_type=MESH,
            ).start()
        return 0

    lax.fori_loop(2, 6, boundary_layer, 0)
    send_chunk(0, first_of(0))

    def bounded(k, _):
        lax.fori_loop(2 * k + 4, 2 * k + 6, boundary_layer, 0)
        return inner(k, 0)

    lax.fori_loop(1, chunks - 3, bounded, 0)

    inner(chunks - 3, 0)

    @pl.when(sp > cross)
    def _():
        pltpu.make_async_copy(relay, relay, relay_sem.at[0]).wait()
        relay_right.start()

    @pl.when(sp < cross - 1)
    def _():
        pltpu.make_async_copy(relay, relay, relay_sem.at[0]).wait()
        relay_left.start()

    lax.fori_loop(0, 1, collide, 0)

    @pl.when(sp > 0)
    def _():
        to_right.wait_recv()

    @pl.when(sp < spaces - 1)
    def _():
        to_left.wait_recv()

    lax.fori_loop(chunks - 2, chunks, inner, 0)

    lax.fori_loop(1, chunks, collide, 0)

    mine = pltpu.make_async_copy(
        done.at[:, own, :], result.at[:, my_y, my_z], own_sem)
    mine.start()

    def finish(k, _):
        x0 = first_of(k)
        block = cells.at[pl.ds(x0, PAIR), pl.ds(0, 240), :]
        pltpu.make_async_copy(block, block, go_send.at[k]).wait()
        pltpu.make_async_copy(block, block, back_send.at[k]).wait()
        pltpu.make_async_copy(block, block, back_recv.at[k]).wait()
        return 0

    lax.fori_loop(0, chunks, finish, 0)
    mine.wait()

    @pl.when(sp > 0)
    def _():
        to_left.wait_send()

    @pl.when(sp < spaces - 1)
    def _():
        to_right.wait_send()

    @pl.when(sp > cross)
    def _():
        relay_right.wait_send()

    @pl.when(sp < cross - 1)
    def _():
        relay_left.wait_send()

    for copy in sends:
        copy.wait_send()


def place_kernel(layers, source, target, held, rows, in_sem, out_sem):
    step = layers // 4

    def load(i):
        return pltpu.make_async_copy(source.at[pl.ds(step * i, step)], held.at[pl.ds(step * i, step)], in_sem.at[i])

    def store(i):
        part = pl.ds(256 * step * i, 256 * step)
        return pltpu.make_async_copy(rows.at[part], target.at[part], out_sem.at[i])

    for i in range(4):
        load(i).start()
    for i in range(4):
        load(i).wait()

        def place(x, _):
            for y in range(4):
                for z in range(4):
                    for e in range(2):
                        rows[pl.ds(256 * x + 64 * y + 32 * e + z, 8, stride=4), :] = held[x, y, z, 8 * e:8 * e + 8, :]
            return 0

        lax.fori_loop(step * i, step * (i + 1), place, 0)
        store(i).start()
    for i in range(4):
        store(i).wait()


def shards(spaces, dist, cell_kind, inflow, wall_shape, gain_tables, second_tables):
    layers = dist.shape[0]
    mats, flips, small = tables()
    rows = dist.reshape(layers, 4, 4, 16, 128).transpose(0, 1, 3, 2, 4).reshape(layers * 256, 128)
    anywhere = pl.BlockSpec(memory_space=pl.ANY)
    chunks = layers // PAIR
    dma = pltpu.SemaphoreType.DMA
    result = pl.pallas_call(
        functools.partial(step_kernel, spaces, layers),
        out_shape=jax.ShapeDtypeStruct((layers, 4, 4, 16, 128), F32),
        in_specs=[anywhere, pl.BlockSpec(memory_space=pltpu.SMEM)] + [anywhere] * 7,
        out_specs=anywhere,
        scratch_shapes=[
            pltpu.VMEM((layers * 256, 128), F32),
            pltpu.VMEM((16, 128), F32), pltpu.VMEM((16, 128), F32),
            pltpu.VMEM((256, 128), F32), pltpu.VMEM((256, 128), F32),
            pltpu.VMEM(mats.shape, F32), pltpu.VMEM(mats.shape, BF16), pltpu.VMEM(mats.shape, BF16), pltpu.VMEM(flips.shape, F32), pltpu.VMEM(small.shape, F32),
            pltpu.VMEM((layers + 4, 4, 4, 16, 128), F32),
            pltpu.VMEM((256, 128), F32),
            pltpu.VMEM((1, 256), F32),
            pltpu.VMEM((16, 1, 256), F32),
            pltpu.VMEM((layers * 16, 128), F32),
            pltpu.VMEM((layers, 16, 16, 128), F32),
            pltpu.VMEM((layers, 256, 128), F32),
            pltpu.VMEM((layers, 256, 128), F32),
            pltpu.VMEM((4, 256, 128), F32),
            pltpu.VMEM((4, HALF, 128), F32),
            pltpu.VMEM((4, 64, 128), F32),
            pltpu.VMEM((4 * PAIR * HALF, 256), BF16),
            pltpu.VMEM((4 * PAIR * HALF, 256), BF16),
            pltpu.VMEM((2, 2, 16, 128), F32),
            dma((8,)), dma((2,)),
            dma((15,)), dma((15,)),
            dma((2,)), dma((2,)),
            dma((chunks,)), dma((chunks,)),
            dma((chunks,)), dma((chunks,)),
            dma,
        ],
        compiler_params=pltpu.CompilerParams(
            collective_id=0, has_side_effects=True, vmem_limit_bytes=56 * 2**20),
    )(
        rows, cell_kind.transpose(1, 2, 0), inflow.reshape(16, 128), wall_shape.reshape(16, 128),
        gain_tables.reshape(256, 128), second_tables.reshape(256, 128),
        jnp.asarray(mats), jnp.asarray(flips), jnp.asarray(small),
    )
    placed = pl.pallas_call(
        functools.partial(place_kernel, layers),
        out_shape=jax.ShapeDtypeStruct((layers * 256, 128), F32),
        in_specs=[anywhere],
        out_specs=anywhere,
        scratch_shapes=[
            pltpu.VMEM((layers, 4, 4, 16, 128), F32), pltpu.VMEM((layers * 256, 128), F32), dma((4,)), dma((4,))],
        compiler_params=pltpu.CompilerParams(vmem_limit_bytes=56 * 2**20),
    )(result)
    return placed.reshape(layers, 4, 16, 4, 128).transpose(0, 1, 3, 2, 4).reshape(dist.shape)


def solution(mesh):
    placed = (P("space", None, None, "vel"), P("space", None, None), P("vel"), P("vel"), P(), P())
    return jax.shard_map(
        functools.partial(shards, mesh.shape["space"]),
        mesh=mesh, in_specs=placed, out_specs=P("space", None, None, "vel"), check_vma=False,
    )
```
